512 devices in a mesh: tm: 16 (over y, core), seq: 32 (over z, x).
Axes of the slice: x: 4, y: 8, z: 8, core: 2. Of those that a mesh axis runs over, the one named last changes fastest.
Arguments:
- trajectory: bfloat16 [16, 4, 1024, 3072], P('tm', None, 'seq'), may hold values from -6 to 6
- plan: int32 [16], P('tm'), may hold values from 0 to 15
- step_sizes: float32 [16], P('tm'), may hold values from 0.05 to 0.5
- modulation: bfloat16 [16, 2, 3, 3072], replicated, may hold values from -3 to 3
- q_gain: float32 [2, 3072], replicated, may hold values from -3.2 to 3.2
- k_gain: float32 [2, 3072], replicated, may hold values from -3.2 to 3.2
- tile_mask: int32 [24, 8, 8], replicated, may hold values from 0 to 1, as said below
Outputs:
- displacement: float32 [16, 4, 1024, 3072], P('tm', None, 'seq')
The draws below stay inside these ranges and needn't reach their ends.
Inputs may be any that keep to these rules, and one draw needn't show every extreme that they name: `tile_mask`: every diagonal tile is kept.
All inputs are finite; a program needn't handle non-finite values.
Results may differ from the reference program's by a relative error of at most 0.0095.
Values may be sent and summed in bfloat16 or wider, within the bound.
A program may use at most 128 MiB of HBM per device.

```python
import math
import jax
import jax.numpy as jnp
from jax import lax

H = 24
HD = 128
D = 3072
TXT = 512
IMG_W = 64
BATCH = 4
TILE = 128
NSCHED = 16
L = 1024
STEPS = 16


def draw_q_gain(key, part):
    key = jax.random.fold_in(key, 1)
    base = jnp.clip(jax.random.normal(key, (2, H * HD), jnp.float32), -3.2, 3.2)
    return base


def draw_k_gain(key, part):
    key = jax.random.fold_in(key, 2)
    base = jnp.clip(jax.random.normal(key, (2, H * HD), jnp.float32), -3.2, 3.2)
    return base


def draw_tile_mask(key, part):
    key = jax.random.fold_in(key, 3)
    tiles = L // TILE
    bits = jax.random.randint(key, (H, tiles, tiles), 0, 2)
    diagonal = (jnp.arange(tiles)[:, None] == jnp.arange(tiles)[None]).astype(jnp.int32)
    return jnp.maximum(bits, diagonal[None]).astype(jnp.int32)


def plant(drawn, rng, low, largest):
    extent = drawn.shape
    index_at = [jax.random.randint(jax.random.fold_in(rng, axis), (), 0, extent[axis]) for axis in range(len(extent))]
    drawn = drawn.at[tuple(index_at)].set(low)
    longest = extent.index(max(extent))
    index_at[longest] = (index_at[longest] + 1) % extent[longest]
    return drawn.at[tuple(index_at)].set(largest)


def levels(rng, dims, shards, least, high):
    def one(axis_at, parts):
        heights = jax.random.uniform(jax.random.fold_in(jax.random.fold_in(rng, 6), axis_at), (parts,), jnp.float32, least / len(shards), high / len(shards))
        return jnp.repeat(jnp.exp(heights), dims[axis_at] // parts).reshape((-1,) + (1,) * (len(dims) - axis_at - 1))

    loudness = one(*shards[0])
    for cut in shards[1:]:
        loudness = loudness * one(*cut)
    return loudness


def centred(rng, extent, width, reach, pieces=(), kind=jnp.bfloat16):
    drawn = width * jax.random.normal(rng, extent, jnp.float32)
    if pieces:
        drawn = drawn * levels(rng, extent, pieces, -0.22, 0.18)
    return jnp.clip(drawn, -reach, reach).astype(kind)


def setup_inputs(seed: int = 0) -> dict:
    key_list = jax.random.split(jax.random.key(seed), 8)
    trajectory = centred(key_list[0], (STEPS, BATCH, L, D), 1.0, 6.0, ((0, 16), (2, 32)))
    plan = plant(jax.random.randint(key_list[1], (STEPS,), 0, NSCHED), jax.random.fold_in(key_list[1], 1), 0, NSCHED - 1).astype(jnp.int32)
    step_sizes = jnp.clip(jnp.exp(math.log(0.5) - 2.3025851 * jax.random.uniform(key_list[2], (STEPS,), jnp.float32) ** levels(key_list[2], (STEPS,), ((0, 16),), -0.2, 0.2)), 0.05, 0.5)
    modulation = centred(key_list[3], (NSCHED, 2, 3, D), 0.5, 3.0)
    q_gain = draw_q_gain(jax.random.fold_in(key_list[7], 71), 0)
    k_gain = draw_k_gain(jax.random.fold_in(key_list[7], 71), 0)
    tile_mask = draw_tile_mask(jax.random.fold_in(key_list[7], 71), 0)
    return {"trajectory": trajectory, "plan": plan, "step_sizes": step_sizes, "modulation": modulation, "q_gain": q_gain, "k_gain": k_gain, "tile_mask": tile_mask}


def rope_tables(positions):
    half = HD // 2
    first = HD // 16
    second = (half - first) // 2
    image = positions - TXT
    is_image = positions >= TXT
    row_pos = jnp.where(is_image, image // IMG_W, 0).astype(jnp.float32)
    col_pos = jnp.where(is_image, image % IMG_W, 0).astype(jnp.float32)
    freqs = 10000.0 ** (-(jnp.arange(second, dtype=jnp.float32) / second))
    angles = jnp.concatenate([jnp.zeros((positions.shape[0], first), jnp.float32), row_pos[:, None] * freqs[None], col_pos[:, None] * freqs[None]], axis=1)
    return (jnp.cos(angles), jnp.sin(angles))

def rotate(values, cosine, sine):
    pairs = values.reshape(values.shape[:-1] + (values.shape[-1] // 2, 2))
    first_part = pairs[..., 0]
    second_part = pairs[..., 1]
    turned = jnp.stack([first_part * cosine - second_part * sine, first_part * sine + second_part * cosine], -1)
    return turned.reshape(values.shape)

def head_norm(values, gain):
    return values * lax.rsqrt(lax.optimization_barrier(jnp.mean(values * values, axis=-1, keepdims=True)) + 1e-06) * gain

def select_rows(table_rows, stream, column):
    return jnp.where(stream[:, None] == 0, table_rows[0, column][None], table_rows[1, column][None])

def modulate(rows, table_rows, stream):
    values = rows.astype(jnp.float32)
    center = lax.optimization_barrier(jnp.mean(values, axis=-1, keepdims=True))
    spread = lax.optimization_barrier(jnp.mean((values - center) ** 2, axis=-1, keepdims=True))
    normed = (values - center) * lax.rsqrt(spread + 1e-06)
    shifted = normed * (1.0 + select_rows(table_rows, stream, 1)) + select_rows(table_rows, stream, 0)
    return (shifted.astype(jnp.bfloat16), select_rows(table_rows, stream, 2))

def attend(query, keys, values, mask_tiles, tile):
    scores = jnp.dot(query, keys.T, preferred_element_type=jnp.float32) * HD ** (-0.5)
    tiles_n = mask_tiles.shape[0]
    scores = scores.reshape(tiles_n, tile, tiles_n, tile)
    scores = jnp.where(mask_tiles[:, None, :, None] > 0, scores, -1e+30).reshape(tiles_n * tile, tiles_n * tile)
    top = lax.optimization_barrier(jnp.max(scores, axis=-1, keepdims=True))
    weights = jnp.exp(scores - top)
    weights = (weights / lax.optimization_barrier(jnp.sum(weights, axis=-1, keepdims=True))).astype(jnp.bfloat16)
    return jnp.dot(weights, values, preferred_element_type=jnp.float32).astype(jnp.bfloat16)

def reference(trajectory, plan, step_sizes, modulation, q_gain, k_gain, tile_mask):
    positions = jnp.arange(L, dtype=jnp.int32)
    stream = (positions >= TXT).astype(jnp.int32)
    cosine, sine = rope_tables(positions)
    q_tok = jnp.where(stream[:, None] == 0, q_gain[0][None], q_gain[1][None]).reshape(L, H, HD).transpose(1, 0, 2)
    k_tok = jnp.where(stream[:, None] == 0, k_gain[0][None], k_gain[1][None]).reshape(L, H, HD).transpose(1, 0, 2)

    def one_step(inputs):
        rows, index, size = inputs
        table_rows = modulation[index].astype(jnp.float32)
        shifted, gate = modulate(rows, table_rows, stream)
        heads = shifted.reshape(BATCH, L, H, HD).transpose(0, 2, 1, 3)
        values32 = heads.astype(jnp.float32)
        query = rotate(head_norm(values32, q_tok[None]), cosine, sine).astype(jnp.bfloat16)
        keys = rotate(head_norm(values32, k_tok[None]), cosine, sine).astype(jnp.bfloat16)

        def one_image(items):
            q_one, k_one, v_one = items
            return lax.map(lambda g: attend(g[0], g[1], g[2], g[3], TILE), (q_one, k_one, v_one, tile_mask))
        attended = lax.map(one_image, (query, keys, heads))
        merged = attended.transpose(0, 2, 1, 3).reshape(BATCH, L, D).astype(jnp.float32)
        return size * gate[None] * merged
    terms = lax.map(one_step, (trajectory, plan, step_sizes))
    return jnp.cumsum(terms, axis=0)
```

```python
import functools

import jax
import jax.numpy as jnp
import numpy as np
from jax import lax
from jax.experimental import pallas as pl
from jax.experimental.pallas import tpu as pltpu
from jax.sharding import PartitionSpec as P

TXT = 512
IMG_W = 64
MESH = pl.DeviceIdType.MESH
F32 = jnp.float32
BF16 = jnp.bfloat16

B, H, HD, D = 4, 24, 128, 3072
L = 1024
S = 32
LOC = L // S
PER = B * H // S
HG = H // PER
HALF = L // 2
CH = 128
NCH = HALF // CH
QB = 256
NEG = -1e30


def rope_tables():
    half = HD // 2
    first = HD // 16
    second = (half - first) // 2
    image = np.arange(L - TXT)
    freqs = (np.float32(10000.0) ** (-(np.arange(second, dtype=np.float32) / np.float32(second)))).astype(np.float32)
    row = (image // IMG_W).astype(np.float32)
    col = (image % IMG_W).astype(np.float32)
    angles = np.concatenate(
        [np.zeros((L - TXT, first), np.float32), row[:, None] * freqs[None], col[:, None] * freqs[None]], axis=1
    ).astype(np.float32)
    cosine = np.repeat(np.cos(angles), 2, axis=1)
    sine = np.repeat(np.sin(angles), 2, axis=1)
    sine[:, 0::2] *= -1.0
    return cosine.astype(np.float32), sine.astype(np.float32)


def kernel(
    plan_ref,
    step_ref,
    x_ref,
    mod_ref,
    qg_ref,
    kg_ref,
    mask_ref,
    cos_ref,
    sin_ref,
    out_ref,
    send_u,
    recv_u,
    q_aug,
    k_aug,
    v_aug,
    bias,
    own,
    ex_out,
    ex_in,
    e_in,
    r_in,
    t_in,
    p_out,
    s_out,
    d_out,
    in_send,
    in_recv,
    ex_send,
    ex_recv,
    f_send,
    f_recv,
    r_send,
    r_recv,
    t_send,
    t_recv,
    o_send,
    o_recv,
):
    tm = lax.axis_index("tm")
    s = lax.axis_index("seq")
    y = tm // 2
    c = tm % 2
    x = s % 4
    image = s // HG
    head0 = (s % HG) * PER
    ypos = y % 4

    bar = pltpu.get_barrier_semaphore()

    def greet(i, carry):
        pl.semaphore_signal(bar, inc=1, device_id=(tm, lax.rem(s + i, S)), device_id_type=MESH)
        return carry

    lax.fori_loop(1, S, greet, 0)

    def greet_tm(other):
        pl.semaphore_signal(bar, inc=1, device_id=(other, s), device_id_type=MESH)

    greet_tm(y * 2 + 1 - c)
    one = jnp.int32(1)
    zero = jnp.int32(0)

    @pl.when(ypos > 0)
    def _():
        greet_tm(tm - 2)

    @pl.when(y < 3)
    def _():
        greet_tm(tm + 2)

    @pl.when((y == 4) | (y == 5))
    def _():
        greet_tm(6 + c)

    @pl.when(y >= 6)
    def _():
        greet_tm(c)

    plan = plan_ref[0]
    stream = jnp.where(s >= TXT // LOC, one, zero)
    table = mod_ref[plan, stream].astype(F32)
    shift = table[0:1]
    scale = 1.0 + table[1:2]

    def modulate(b, carry):
        rows = x_ref[b].astype(F32)
        center = jnp.mean(rows, axis=-1, keepdims=True)
        rows = rows - center
        spread = jnp.mean(rows * rows, axis=-1, keepdims=True)
        u = (rows * lax.rsqrt(spread + 1e-06) * scale + shift).astype(BF16)
        for h in range(H):
            send_u[b * HG + h // PER, h % PER] = u[:, h * HD : (h + 1) * HD]
        return carry

    lax.fori_loop(0, B, modulate, 0)

    receivers = 31 + 1 + jnp.where(ypos != 3, one, zero) + jnp.where((y >= 1) & (y <= 3), one, zero)
    receivers = receivers + jnp.where((y == 0) | (y == 3), one + one, zero)
    pl.semaphore_wait(bar, receivers)

    for j in range(PER):
        pltpu.make_async_copy(send_u.at[s, j], recv_u.at[j, s], in_recv.at[j]).start()

        def spread_u(i, carry, j=j):
            p = lax.rem(s + i, S)
            pltpu.make_async_remote_copy(
                send_u.at[p, j],
                recv_u.at[j, s],
                in_send,
                in_recv.at[j],
                device_id=(tm, p),
                device_id_type=MESH,
            ).start()
            return carry

        lax.fori_loop(1, S, spread_u, 0)

    lane = lax.broadcasted_iota(jnp.int32, (L, HD), 1)
    tile = lax.broadcasted_iota(jnp.int32, (L, HD), 0) // 128
    k_aug[:, HD:] = jnp.where(lane == tile, 1.0, 0.0).astype(BF16)
    v_aug[:, HD:] = jnp.ones((L, HD), BF16)
    bias[...] = jnp.zeros((8, HD), F32)
    lane_row = lax.broadcasted_iota(jnp.int32, (HD, HD), 0)
    lane_col = lax.broadcasted_iota(jnp.int32, (HD, HD), 1)
    partner = jnp.where(lane_col % 2 == 0, lane_col + 1, lane_col - 1)
    swap = jnp.where(lane_row == partner, 1.0, 0.0).astype(BF16)
    even = lax.broadcasted_iota(jnp.int32, (8, HD), 1) % 2 == 0
    factor = HD ** (-0.5) * 1.4426950408889634
    step = step_ref[0]

    def swapped(row):
        row = jnp.broadcast_to(row, (8, HD))
        return jnp.where(even, pltpu.roll(row, HD - 1, 1), pltpu.roll(row, 1, 1))[0:1]

    def attention(j):
        head = head0 + j
        cols = pl.ds(pl.multiple_of(head * HD, HD), HD)
        pltpu.make_async_copy(recv_u.at[j], recv_u.at[j], in_recv.at[j]).wait()
        u = recv_u[j].reshape(L, HD)
        v_aug[:, :HD] = u
        u32 = u.astype(F32)
        inv = lax.rsqrt(jnp.mean(u32 * u32, axis=-1, keepdims=True) + 1e-06)
        n32 = u32 * inv
        turned = jnp.dot(u[TXT:], swap, preferred_element_type=F32) * inv[TXT:]
        cosine = cos_ref[...]
        sine = sin_ref[...]

        def fill(target, gain_ref, extra):
            gain = gain_ref[:, cols] * extra
            target[:TXT, :HD] = (n32[:TXT] * gain[0:1]).astype(BF16)
            target[TXT:, :HD] = (
                n32[TXT:] * (cosine * gain[1:2]) + turned * (sine * swapped(gain[1:2]))
            ).astype(BF16)

        fill(q_aug, qg_ref, factor)
        fill(k_aug, kg_ref, 1.0)
        kept = mask_ref[head].astype(F32)
        bias[:, 0:8] = (1.0 - kept) * NEG
        for a in range(8):
            q_aug[a * 128 : (a + 1) * 128, HD:] = jnp.broadcast_to(bias[a : a + 1, :], (128, HD)).astype(BF16)

        gate_text = mod_ref[plan, 0, :, cols].astype(F32)[2:3] * step
        gate_image = mod_ref[plan, 1, :, cols].astype(F32)[2:3] * step

        def rows_of(start, is_image):
            query = q_aug[pl.ds(start, QB), :]
            scores = lax.dot_general(query, k_aug[...], (((1,), (1,)), ((), ())), preferred_element_type=F32)
            top = jnp.max(scores, axis=-1, keepdims=True)
            weights = jnp.exp2(scores - top).astype(BF16)
            summed = jnp.dot(weights, v_aug[...], preferred_element_type=F32)
            gate = jnp.where(is_image, gate_image, gate_text)
            return (summed[:, :HD] / summed[:, HD:]) * gate

        for n in range(HALF // QB):
            theirs = pl.multiple_of((1 - c) * HALF + n * QB, QB)
            ex_out[j, n] = rows_of(theirs, c == 0).astype(BF16)
            pltpu.make_async_remote_copy(
                ex_out.at[j, n],
                ex_in.at[j, n],
                ex_send.at[j, n],
                ex_recv.at[j, n],
                device_id=(y * 2 + 1 - c, s),
                device_id_type=MESH,
            ).start()
        for n in range(HALF // QB):
            mine = pl.multiple_of(c * HALF + n * QB, QB)
            own[j, n * QB : (n + 1) * QB] = rows_of(mine, c == 1)
        for n in range(HALF // QB):
            pltpu.make_async_remote_copy(
                ex_out.at[j, n],
                ex_in.at[j, n],
                ex_send.at[j, n],
                ex_recv.at[j, n],
                device_id=(y * 2 + 1 - c, s),
                device_id_type=MESH,
            ).wait()

    def chunk_of(i):
        return lax.rem(i + x, NCH)

    def both(j, r):
        mine = own[j, pl.ds(pl.multiple_of(r * CH, CH), CH), :]
        other = ex_in[j, r // 2, pl.ds(pl.multiple_of((r % 2) * CH, CH), CH), :].astype(F32)
        return mine, other

    def hop(src, dst, send_sem, recv_sem, to):
        return pltpu.make_async_remote_copy(src, dst, send_sem, recv_sem, device_id=(to, s), device_id_type=MESH)

    def forward_copy(g):
        return hop(p_out.at[g], e_in.at[g], f_send.at[g], f_recv.at[g], tm + 2)

    def reverse_copy(g):
        return hop(s_out.at[g], r_in.at[g], r_send.at[g], r_recv.at[g], tm - 2)

    def total_copy(src, g, n):
        to = jnp.where(y == 3, 8 + 2 * n, 14 - 2 * n) + c
        return hop(src.at[g], t_in.at[g], t_send.at[n, g], t_recv.at[g], to)

    def forward(j):
        def one_chunk(i, carry):
            r = chunk_of(i)
            g = j * NCH + r
            mine, other = both(j, r)
            total = mine + other

            @pl.when(ypos == 0)
            def _():
                p_out[g] = total.astype(BF16)

            @pl.when(ypos > 0)
            def _():
                forward_copy(g).wait_recv()
                p_out[g] = (total + e_in[g].astype(F32)).astype(BF16)

            @pl.when(ypos < 3)
            def _():
                forward_copy(g).start()

            @pl.when(y == 3)
            def _():
                total_copy(p_out, g, 0).start()
                total_copy(p_out, g, 1).start()
                s_out[g] = total.astype(BF16)
                reverse_copy(g).start()

            return carry

        lax.fori_loop(0, NCH, one_chunk, 0)

    def reverse(j):
        @pl.when(y < 3)
        def _():
            def one_chunk(i, carry):
                r = chunk_of(i)
                g = j * NCH + r
                mine, other = both(j, r)
                reverse_copy(g).wait_recv()
                s_out[g] = (mine + other + r_in[g].astype(F32)).astype(BF16)

                @pl.when(y > 0)
                def _():
                    reverse_copy(g).start()

                @pl.when(y == 0)
                def _():
                    total_copy(s_out, g, 0).start()
                    total_copy(s_out, g, 1).start()

                return carry

            lax.fori_loop(0, NCH, one_chunk, 0)

    def deliver(j):
        cols = pl.ds(pl.multiple_of((head0 + j) * HD, HD), HD)

        def one_chunk(i, carry):
            r = chunk_of(i)
            g = j * NCH + r
            mine, other = both(j, r)

            def put(before):
                after = before + mine + other
                first = before + jnp.where(c == 0, mine, other)
                d_out[0, g] = first.astype(BF16)
                d_out[1, g] = after.astype(BF16)

            @pl.when(y == 0)
            def _():
                put(jnp.zeros((CH, HD), F32))

            @pl.when((y > 0) & (y < 4))
            def _():
                put(e_in[g].astype(F32))

            @pl.when(y >= 4)
            def _():
                total_copy(p_out, g, 0).wait_recv()

            @pl.when(y == 4)
            def _():
                put(t_in[g].astype(F32))

            @pl.when(y > 4)
            def _():
                put(t_in[g].astype(F32) + e_in[g].astype(F32))

            def piece(i, carry):
                step_to = y * 2 + i // 4
                shard = c * (S // 2) + r * 4 + lax.rem(i + s // 4, 4)
                src = d_out.at[i // 4, g, pl.ds(pl.multiple_of(lax.rem(i + s // 4, 4) * LOC, LOC), LOC)]
                dst = out_ref.at[image, :, cols]
                here = (shard == s) & (step_to == tm)

                @pl.when(here)
                def _():
                    pltpu.make_async_copy(src, dst, o_recv).start()

                @pl.when(jnp.logical_not(here))
                def _():
                    pltpu.make_async_remote_copy(
                        src, dst, o_send, o_recv, device_id=(step_to, shard), device_id_type=MESH
                    ).start()

                return carry

            lax.fori_loop(0, 8, piece, 0)
            return carry

        lax.fori_loop(0, NCH, one_chunk, 0)

    attention(0)
    forward(0)
    attention(1)
    forward(1)
    reverse(0)

    @pl.when(y < 4)
    def _():
        deliver(0)

    attention(2)
    forward(2)

    @pl.when(y >= 4)
    def _():
        deliver(0)

    reverse(1)
    deliver(1)
    reverse(2)
    deliver(2)

    sent = send_u.at[pl.ds(0, S - 1)]
    pltpu.make_async_copy(sent, sent, in_send).wait()

    def drain(g, carry):
        @pl.when(ypos < 3)
        def _():
            forward_copy(g).wait_send()

        @pl.when((y >= 1) & (y <= 3))
        def _():
            reverse_copy(g).wait_send()

        @pl.when((y == 0) | (y == 3))
        def _():
            total_copy(p_out, g, 0).wait_send()
            total_copy(p_out, g, 1).wait_send()

        return carry

    lax.fori_loop(0, PER * NCH, drain, 0)
    most = d_out.at[0, :, pl.ds(0, CH - LOC)]
    pltpu.make_async_copy(d_out.at[1], d_out.at[1], o_send).wait()
    pltpu.make_async_copy(most, most, o_send).wait()
    rest = d_out.at[0, :, pl.ds(0, LOC)]
    last = d_out.at[0, pl.ds(0, 9), pl.ds(0, LOC)]
    holds_own = c == s // (S // 2)

    @pl.when(holds_own)
    def _():
        pltpu.make_async_copy(last, last, o_send).wait()

    @pl.when(jnp.logical_not(holds_own))
    def _():
        pltpu.make_async_copy(rest, rest, o_send).wait()

    pltpu.make_async_copy(out_ref, out_ref, o_recv).wait()


def body(trajectory, plan, step_sizes, modulation, q_gain, k_gain, tile_mask):
    cosine, sine = rope_tables()
    n = PER * NCH
    vmem = pl.BlockSpec(memory_space=pltpu.VMEM)
    smem = pl.BlockSpec(memory_space=pltpu.SMEM)
    dma = pltpu.SemaphoreType.DMA
    blocks = pl.pallas_call(
        kernel,
        out_shape=jax.ShapeDtypeStruct((B, LOC, D), BF16),
        in_specs=[smem, smem] + [vmem] * 7,
        out_specs=pl.BlockSpec(memory_space=pl.ANY),
        scratch_shapes=[
            pltpu.VMEM((S, PER, LOC, HD), BF16),
            pltpu.VMEM((PER, S, LOC, HD), BF16),
            pltpu.VMEM((L, 2 * HD), BF16),
            pltpu.VMEM((L, 2 * HD), BF16),
            pltpu.VMEM((L, 2 * HD), BF16),
            pltpu.VMEM((8, HD), F32),
            pltpu.VMEM((PER, HALF, HD), F32),
            pltpu.VMEM((PER, HALF // QB, QB, HD), BF16),
            pltpu.VMEM((PER, HALF // QB, QB, HD), BF16),
            pltpu.VMEM((n, CH, HD), BF16),
            pltpu.VMEM((n, CH, HD), BF16),
            pltpu.VMEM((n, CH, HD), BF16),
            pltpu.VMEM((n, CH, HD), BF16),
            pltpu.VMEM((n, CH, HD), BF16),
            pltpu.VMEM((2, n, CH, HD), BF16),
            dma,
            dma((PER,)),
            dma((PER, HALF // QB)),
            dma((PER, HALF // QB)),
            dma((n,)),
            dma((n,)),
            dma((n,)),
            dma((n,)),
            dma((2, n)),
            dma((n,)),
            dma,
            dma,
        ],
        compiler_params=pltpu.CompilerParams(
            collective_id=0, has_side_effects=True, vmem_limit_bytes=56 * 1024 * 1024
        ),
    )(plan, step_sizes, trajectory[0], modulation, q_gain, k_gain, tile_mask, jnp.asarray(cosine), jnp.asarray(sine))
    return blocks.astype(F32)[None]


def solution(mesh):
    placed = (P("tm", None, "seq", None), P("tm"), P("tm"), P(), P(), P(), P())
    return jax.shard_map(
        body, mesh=mesh, in_specs=placed, out_specs=P("tm", None, "seq", None), check_vma=False
    )
```

```python
import functools

import jax
import jax.numpy as jnp
import numpy as np
from jax import lax
from jax.experimental import pallas as pl
from jax.experimental.pallas import tpu as pltpu
from jax.sharding import PartitionSpec as P

TXT = 512
IMG_W = 64
MESH = pl.DeviceIdType.MESH
F32 = jnp.float32
BF16 = jnp.bfloat16

B, H, HD, D = 4, 24, 128, 3072
L = 1024
S = 32
LOC = L // S
PER = B * H // S
HG = H // PER
HALF = L // 2
CH = 128
NCH = HALF // CH
QB = 256
NEG = -1e30

TO = {0: (1, 6, 7), 1: (0, 2, 3), 2: (0, 3), 3: (2, 4, 5), 4: (5,), 5: (6, 7), 6: (7,)}


def rope_tables():
    half = HD // 2
    first = HD // 16
    second = (half - first) // 2
    image = np.arange(L - TXT)
    freqs = (np.float32(10000.0) ** (-(np.arange(second, dtype=np.float32) / np.float32(second)))).astype(np.float32)
    row = (image // IMG_W).astype(np.float32)
    col = (image % IMG_W).astype(np.float32)
    angles = np.concatenate(
        [np.zeros((L - TXT, first), np.float32), row[:, None] * freqs[None], col[:, None] * freqs[None]], axis=1
    ).astype(np.float32)
    cosine = np.repeat(np.cos(angles), 2, axis=1)
    sine = np.repeat(np.sin(angles), 2, axis=1)
    sine[:, 0::2] *= -1.0
    return cosine.astype(np.float32), sine.astype(np.float32)


def kernel(
    plan_ref,
    step_ref,
    x_hbm,
    mod_hbm,
    qg_hbm,
    kg_hbm,
    mask_hbm,
    cos_hbm,
    sin_hbm,
    out_ref,
    x_ref,
    mod_ref,
    qg_ref,
    kg_ref,
    mask_ref,
    cos_ref,
    sin_ref,
    send_u,
    recv_u,
    q_aug,
    k_aug,
    v_aug,
    own,
    ex_out,
    ex_in,
    a_in,
    b_in,
    r_in,
    t_in,
    c_out,
    p_out,
    t_out,
    d_out,
    in_send,
    in_recv,
    ex_send,
    ex_recv,
    a_recv,
    b_recv,
    r_recv,
    t_recv,
    c_send,
    p_send,
    t_send,
    o_send,
    o_recv,
    load,
):
    tm = lax.axis_index("tm")
    s = lax.axis_index("seq")
    y = tm // 2
    c = tm % 2
    x = s % 4
    image = s // HG
    head0 = (s % HG) * PER
    ypos = y % 4

    loads = [
        pltpu.make_async_copy(src, dst, load.at[n])
        for n, (src, dst) in enumerate(
            [
                (x_hbm, x_ref),
                (mod_hbm, mod_ref),
                (qg_hbm, qg_ref),
                (kg_hbm, kg_ref),
                (mask_hbm, mask_ref),
                (cos_hbm, cos_ref),
                (sin_hbm, sin_ref),
            ]
        )
    ]
    for copy in loads:
        copy.start()

    bar = pltpu.get_barrier_semaphore()

    def greet(i, carry):
        pl.semaphore_signal(bar, inc=1, device_id=(tm, lax.rem(s + i, S)), device_id_type=MESH)
        return carry

    lax.fori_loop(1, S, greet, 0)

    def greet_tm(other):
        pl.semaphore_signal(bar, inc=1, device_id=(other, s), device_id_type=MESH)

    greet_tm(y * 2 + 1 - c)
    zero = jnp.int32(0)

    for sender, receivers in TO.items():
        for receiver in receivers:

            @pl.when(y == receiver)
            def _(sender=sender):
                greet_tm(2 * sender + c)

    loads[0].wait()
    loads[1].wait()
    plan = plan_ref[0]
    stream = jnp.where(s >= TXT // LOC, jnp.int32(1), zero)
    table = mod_ref[plan].astype(F32)
    text = stream == 0
    shift = jnp.where(text, table[0, 0:1], table[0, 1:2])
    scale = 1.0 + jnp.where(text, table[1, 0:1], table[1, 1:2])

    def modulate(b, carry):
        rows = x_ref[b].astype(F32)
        center = jnp.mean(rows, axis=-1, keepdims=True)
        rows = rows - center
        spread = jnp.mean(rows * rows, axis=-1, keepdims=True)
        u = (rows * lax.rsqrt(spread + 1e-06) * scale + shift).astype(BF16)
        for h in range(H):
            send_u[b * HG + h // PER, h % PER] = u[:, h * HD : (h + 1) * HD]
        return carry

    lax.fori_loop(0, B, modulate, 0)

    expected = S - 1 + 1
    for sender, receivers in TO.items():
        expected = expected + jnp.where(y == sender, jnp.int32(len(receivers)), zero)
    pl.semaphore_wait(bar, expected)

    for j in range(PER):
        pltpu.make_async_copy(send_u.at[s, j], recv_u.at[j, s], in_recv.at[j]).start()

        def spread_u(i, carry, j=j):
            p = lax.rem(s + i, S)
            pltpu.make_async_remote_copy(
                send_u.at[p, j],
                recv_u.at[j, s],
                in_send,
                in_recv.at[j],
                device_id=(tm, p),
                device_id_type=MESH,
            ).start()
            return carry

        lax.fori_loop(1, S, spread_u, 0)

    for copy in loads[2:]:
        copy.wait()

    lane = lax.broadcasted_iota(jnp.int32, (L, HD), 1)
    tile = lax.broadcasted_iota(jnp.int32, (L, HD), 0) // 128
    q_aug[:, HD:] = jnp.where(lane == tile, 1.0, 0.0).astype(BF16)
    v_aug[:, HD:] = jnp.ones((L, HD), BF16)
    lane_row = lax.broadcasted_iota(jnp.int32, (HD, HD), 0)
    lane_col = lax.broadcasted_iota(jnp.int32, (HD, HD), 1)
    partner = jnp.where(lane_col % 2 == 0, lane_col + 1, lane_col - 1)
    swap = jnp.where(lane_row == partner, 1.0, 0.0).astype(BF16)
    even = lax.broadcasted_iota(jnp.int32, (8, HD), 1) % 2 == 0
    factor = HD ** (-0.5) * 1.4426950408889634
    step = step_ref[0]

    def swapped(row):
        row = jnp.broadcast_to(row, (8, HD))
        return jnp.where(even, pltpu.roll(row, HD - 1, 1), pltpu.roll(row, 1, 1))[0:1]

    def attention(j):
        head = head0 + j
        cols = pl.ds(pl.multiple_of(head * HD, HD), HD)
        pltpu.make_async_copy(recv_u.at[j], recv_u.at[j], in_recv.at[j]).wait()
        u = recv_u[j].reshape(L, HD)
        v_aug[:, :HD] = u
        u32 = u.astype(F32)
        inv = lax.rsqrt(jnp.mean(u32 * u32, axis=-1, keepdims=True) + 1e-06)
        n32 = u32 * inv
        turned = jnp.dot(u[TXT:], swap, preferred_element_type=F32) * inv[TXT:]
        cosine = cos_ref[...]
        sine = sin_ref[...]

        def fill(target, gain_ref, extra):
            gain = gain_ref[:, cols] * extra
            target[:TXT, :HD] = (n32[:TXT] * gain[0:1]).astype(BF16)
            target[TXT:, :HD] = (
                n32[TXT:] * (cosine * gain[1:2]) + turned * (sine * swapped(gain[1:2]))
            ).astype(BF16)

        fill(q_aug, qg_ref, factor)
        fill(k_aug, kg_ref, 1.0)
        masks = mask_ref[...].astype(F32)
        of_head = lax.broadcasted_iota(jnp.int32, masks.shape, 2) == head
        kept = jnp.sum(jnp.where(of_head, masks, 0.0), axis=2, keepdims=True)
        lanes = lax.broadcasted_iota(jnp.int32, (8, HD), 1)
        bias = jnp.zeros((8, HD), F32)
        for a in range(8):
            bias = jnp.where(lanes == a, (1.0 - kept[a]) * NEG, bias)
        for b in range(8):
            k_aug[b * 128 : (b + 1) * 128, HD:] = jnp.broadcast_to(bias[b : b + 1, :], (128, HD)).astype(BF16)

        gates = mod_ref[plan, 2, :, cols].astype(F32) * step
        gate_text, gate_image = gates[0:1], gates[1:2]

        def rows_of(start, is_image):
            query = q_aug[pl.ds(start, QB), :]
            scores = lax.dot_general(query, k_aug[...], (((1,), (1,)), ((), ())), preferred_element_type=F32)
            top = jnp.max(scores, axis=-1, keepdims=True)
            weights = jnp.exp2(scores - top).astype(BF16)
            summed = jnp.dot(weights, v_aug[...], preferred_element_type=F32)
            gate = jnp.where(is_image, gate_image, gate_text)
            return (summed[:, :HD] / summed[:, HD:]) * gate

        for n in range(HALF // QB):
            theirs = pl.multiple_of((1 - c) * HALF + n * QB, QB)
            ex_out[j, n] = rows_of(theirs, c == 0).astype(BF16)
            pltpu.make_async_remote_copy(
                ex_out.at[j, n],
                ex_in.at[j, n],
                ex_send.at[j, n],
                ex_recv.at[j, n],
                device_id=(y * 2 + 1 - c, s),
                device_id_type=MESH,
            ).start()
        for n in range(HALF // QB):
            mine = pl.multiple_of(c * HALF + n * QB, QB)
            own[j, n * QB : (n + 1) * QB] = rows_of(mine, c == 1)

    def chunk_of(i):
        return lax.rem(i + x, NCH)

    def both(j, r):
        mine = own[j, pl.ds(pl.multiple_of(r * CH, CH), CH), :]
        other = ex_in[j, r // 2, pl.ds(pl.multiple_of((r % 2) * CH, CH), CH), :].astype(F32)
        return mine, other

    def hop(src, dst, send_sem, recv_sem, to):
        return pltpu.make_async_remote_copy(src, dst, send_sem, recv_sem, device_id=(to, s), device_id_type=MESH)

    def push_copy(g, dst, recv, to):
        return hop(c_out.at[g], dst.at[g], c_send.at[g], recv.at[g], 2 * to + c)

    def pair_copy(g, n, dst, recv, to):
        return hop(p_out.at[g], dst.at[g], p_send.at[n, g], recv.at[g], 2 * to + c)

    def total_copy(g, n):
        to = jnp.where(y == 3, 4 + n, 7 - n)
        return hop(t_out.at[g], t_in.at[g], t_send.at[n, g], t_recv.at[g], 2 * to + c)

    def got(recv, g):
        hop(c_out.at[g], a_in.at[g], c_send.at[g], recv.at[g], tm).wait_recv()

    def chunks(j, one_chunk):
        def run(i, carry):
            r = chunk_of(i)
            one_chunk(r, j * NCH + r)
            return carry

        lax.fori_loop(0, NCH, run, 0)

    def push(j):
        for n in range(HALF // QB):
            pltpu.make_async_remote_copy(
                ex_out.at[j, n],
                ex_in.at[j, n],
                ex_send.at[j, n],
                ex_recv.at[j, n],
                device_id=(y * 2 + 1 - c, s),
                device_id_type=MESH,
            ).wait()

        def one_chunk(r, g):
            mine, other = both(j, r)
            c_out[g] = (mine + other).astype(BF16)
            pl.when(ypos == 0)(lambda: push_copy(g, a_in, a_recv, y + 1).start())
            pl.when(ypos == 2)(lambda: push_copy(g, b_in, b_recv, y + 1).start())
            pl.when(y == 3)(lambda: push_copy(g, r_in, r_recv, y - 1).start())
            pl.when(y == 1)(lambda: push_copy(g, a_in, a_recv, y - 1).start())

        chunks(j, one_chunk)

    def middle(j):
        def one_chunk(r, g):
            mine, other = both(j, r)

            @pl.when(ypos == 1)
            def _():
                got(a_recv, g)
                p_out[g] = (mine + other + a_in[g].astype(F32)).astype(BF16)
                pair_copy(g, 0, a_in, a_recv, y + 1).start()
                pair_copy(g, 1, a_in, a_recv, y + 2).start()

            @pl.when(y == 2)
            def _():
                got(r_recv, g)
                p_out[g] = (mine + other + r_in[g].astype(F32)).astype(BF16)
                pair_copy(g, 0, r_in, r_recv, y - 2).start()

        pl.when((ypos == 1) | (y == 2))(lambda: chunks(j, one_chunk))

    def total(j):
        def one_chunk(r, g):
            mine, other = both(j, r)
            got(a_recv, g)
            before = mine + other + a_in[g].astype(F32)

            @pl.when(y == 3)
            def _():
                got(b_recv, g)
                t_out[g] = (before + b_in[g].astype(F32)).astype(BF16)

            @pl.when(y == 0)
            def _():
                got(r_recv, g)
                t_out[g] = (before + r_in[g].astype(F32)).astype(BF16)

            total_copy(g, 0).start()
            total_copy(g, 1).start()

        chunks(j, one_chunk)

    def deliver(j):
        cols = pl.ds(pl.multiple_of((head0 + j) * HD, HD), HD)

        def one_chunk(r, g):
            mine, other = both(j, r)

            def put(before):
                after = before + mine + other
                first = before + jnp.where(c == 0, mine, other)
                d_out[0, g] = first.astype(BF16)
                d_out[1, g] = after.astype(BF16)

            pl.when((ypos == 2) | (y == 7))(lambda: got(a_recv, g))
            pl.when(y == 7)(lambda: got(b_recv, g))
            pl.when(y >= 4)(lambda: got(t_recv, g))

            def put_sum(*refs):
                put(sum(ref[g].astype(F32) for ref in refs))

            pl.when(y == 0)(lambda: put(jnp.zeros((CH, HD), F32)))
            pl.when((y == 1) | (y == 2))(lambda: put_sum(a_in))
            pl.when(y == 3)(lambda: put_sum(a_in, b_in))
            pl.when(y == 4)(lambda: put_sum(t_in))
            pl.when((y == 5) | (y == 6))(lambda: put_sum(t_in, a_in))
            pl.when(y == 7)(lambda: put_sum(t_in, a_in, b_in))

            def piece(i, carry):
                step_to = y * 2 + i // 4
                shard = c * (S // 2) + r * 4 + lax.rem(i + s // 4, 4)
                src = d_out.at[i // 4, g, pl.ds(pl.multiple_of(lax.rem(i + s // 4, 4) * LOC, LOC), LOC)]
                dst = out_ref.at[image, :, cols]
                here = (shard == s) & (step_to == tm)

                @pl.when(here)
                def _():
                    pltpu.make_async_copy(src, dst, o_recv).start()

                @pl.when(jnp.logical_not(here))
                def _():
                    pltpu.make_async_remote_copy(
                        src, dst, o_send, o_recv, device_id=(step_to, shard), device_id_type=MESH
                    ).start()

                return carry

            lax.fori_loop(0, 8, piece, 0)

        chunks(j, one_chunk)

    attention(0)
    push(0)
    pl.when(y == 1)(lambda: middle(0))
    attention(1)
    pl.when((y == 2) | (y == 5))(lambda: middle(0))
    pl.when(y == 3)(lambda: total(0))
    push(1)
    pl.when(y < 4)(lambda: deliver(0))
    attention(2)
    pl.when(y == 1)(lambda: middle(1))
    push(2)
    pl.when((y == 2) | (y == 5))(lambda: middle(1))
    pl.when(y == 0)(lambda: total(0))
    pl.when(y == 3)(lambda: total(1))
    pl.when(y >= 4)(lambda: deliver(0))
    pl.when(y != 5)(lambda: deliver(1))
    pl.when(y == 0)(lambda: deliver(2))
    middle(2)
    pl.when(y == 3)(lambda: total(2))
    pl.when(y == 0)(lambda: total(1))
    pl.when(y == 0)(lambda: total(2))
    pl.when(y == 5)(lambda: deliver(1))
    pl.when(y > 0)(lambda: deliver(2))

    sent = send_u.at[pl.ds(0, S - 1)]
    pltpu.make_async_copy(sent, sent, in_send).wait()

    def drain(g, carry):
        pl.when((ypos == 0) | (ypos == 2) | (y == 1) | (y == 3))(
            lambda: push_copy(g, a_in, a_recv, y).wait_send()
        )
        pl.when((ypos == 1) | (y == 2))(lambda: pair_copy(g, 0, a_in, a_recv, y).wait_send())
        pl.when(ypos == 1)(lambda: pair_copy(g, 1, a_in, a_recv, y).wait_send())

        @pl.when((y == 0) | (y == 3))
        def _():
            total_copy(g, 0).wait_send()
            total_copy(g, 1).wait_send()

        return carry

    lax.fori_loop(0, PER * NCH, drain, 0)
    most = d_out.at[0, :, pl.ds(0, CH - LOC)]
    pltpu.make_async_copy(d_out.at[1], d_out.at[1], o_send).wait()
    pltpu.make_async_copy(most, most, o_send).wait()
    rest = d_out.at[0, :, pl.ds(0, LOC)]
    last = d_out.at[0, pl.ds(0, 9), pl.ds(0, LOC)]
    holds_own = c == s // (S // 2)

    @pl.when(holds_own)
    def _():
        pltpu.make_async_copy(last, last, o_send).wait()

    @pl.when(jnp.logical_not(holds_own))
    def _():
        pltpu.make_async_copy(rest, rest, o_send).wait()

    pltpu.make_async_copy(out_ref, out_ref, o_recv).wait()


def body(trajectory, plan, step_sizes, modulation, q_gain, k_gain, tile_mask):
    cosine, sine = rope_tables()
    n = PER * NCH
    smem = pl.BlockSpec(memory_space=pltpu.SMEM)
    dma = pltpu.SemaphoreType.DMA
    blocks = pl.pallas_call(
        kernel,
        out_shape=jax.ShapeDtypeStruct((B, LOC, D), BF16),
        in_specs=[smem, smem] + [pl.BlockSpec(memory_space=pl.ANY)] * 7,
        out_specs=pl.BlockSpec(memory_space=pl.ANY),
        scratch_shapes=[
            pltpu.VMEM((B, LOC, D), BF16),
            pltpu.VMEM((modulation.shape[0], 3, 2, D), BF16),
            pltpu.VMEM((2, D), F32),
            pltpu.VMEM((2, D), F32),
            pltpu.VMEM((L // 128, L // 128, H), jnp.int32),
            pltpu.VMEM((L - TXT, HD), F32),
            pltpu.VMEM((L - TXT, HD), F32),
            pltpu.VMEM((S, PER, LOC, HD), BF16),
            pltpu.VMEM((PER, S, LOC, HD), BF16),
            pltpu.VMEM((L, 2 * HD), BF16),
            pltpu.VMEM((L, 2 * HD), BF16),
            pltpu.VMEM((L, 2 * HD), BF16),
            pltpu.VMEM((PER, HALF, HD), F32),
            pltpu.VMEM((PER, HALF // QB, QB, HD), BF16),
            pltpu.VMEM((PER, HALF // QB, QB, HD), BF16),
            pltpu.VMEM((n, CH, HD), BF16),
            pltpu.VMEM((n, CH, HD), BF16),
            pltpu.VMEM((n, CH, HD), BF16),
            pltpu.VMEM((n, CH, HD), BF16),
            pltpu.VMEM((n, CH, HD), BF16),
            pltpu.VMEM((n, CH, HD), BF16),
            pltpu.VMEM((n, CH, HD), BF16),
            pltpu.VMEM((2, n, CH, HD), BF16),
            dma,
            dma((PER,)),
            dma((PER, HALF // QB)),
            dma((PER, HALF // QB)),
            dma((n,)),
            dma((n,)),
            dma((n,)),
            dma((n,)),
            dma((n,)),
            dma((2, n)),
            dma((2, n)),
            dma,
            dma,
            dma((7,)),
        ],
        compiler_params=pltpu.CompilerParams(
            collective_id=0, has_side_effects=True, vmem_limit_bytes=56 * 1024 * 1024
        ),
    )(plan, step_sizes, trajectory[0], modulation.transpose(0, 2, 1, 3), q_gain, k_gain, tile_mask.transpose(1, 2, 0), jnp.asarray(cosine), jnp.asarray(sine))
    return blocks.astype(F32)[None]


def solution(mesh):
    placed = (P("tm", None, "seq", None), P("tm"), P("tm"), P(), P(), P(), P())
    return jax.shard_map(
        body, mesh=mesh, in_specs=placed, out_specs=P("tm", None, "seq", None), check_vma=False
    )
```

```python
import functools

import jax
import jax.numpy as jnp
import numpy as np
from jax import lax
from jax.experimental import pallas as pl
from jax.experimental.pallas import tpu as pltpu
from jax.sharding import PartitionSpec as P

TXT = 512
IMG_W = 64
MESH = pl.DeviceIdType.MESH
F32 = jnp.float32
BF16 = jnp.bfloat16

B, H, HD, D = 4, 24, 128, 3072
L = 1024
S = 32
LOC = L // S
PER = B * H // S
HG = H // PER
HALF = L // 2
CH = 128
NCH = HALF // CH
NEG = -1e30

TO = {0: (1,), 1: (2, 3, 6, 7), 2: (1, 3), 3: (1, 4, 5), 4: (5,), 5: (6, 7), 6: (7,)}


def rope_tables():
    half = HD // 2
    first = HD // 16
    second = (half - first) // 2
    image = np.arange(L - TXT)
    freqs = (np.float32(10000.0) ** (-(np.arange(second, dtype=np.float32) / np.float32(second)))).astype(np.float32)
    row = (image // IMG_W).astype(np.float32)
    col = (image % IMG_W).astype(np.float32)
    angles = np.concatenate(
        [np.zeros((L - TXT, first), np.float32), row[:, None] * freqs[None], col[:, None] * freqs[None]], axis=1
    ).astype(np.float32)
    cosine = np.repeat(np.cos(angles), 2, axis=1)
    sine = np.repeat(np.sin(angles), 2, axis=1)
    sine[:, 0::2] *= -1.0
    return cosine.astype(np.float32), sine.astype(np.float32)


def kernel(
    plan_ref,
    step_ref,
    x_hbm,
    mod_hbm,
    qg_hbm,
    kg_hbm,
    mask_hbm,
    cos_hbm,
    sin_hbm,
    out_ref,
    x_ref,
    mod_ref,
    qg_ref,
    kg_ref,
    mask_ref,
    cos_ref,
    sin_ref,
    send_u,
    recv_u,
    q_aug,
    k_aug,
    v_aug,
    own,
    ex_out,
    ex_in,
    a_in,
    b_in,
    r_in,
    t_in,
    c_out,
    p_out,
    t_out,
    d_out,
    in_send,
    in_recv,
    ex_send,
    ex_recv,
    a_recv,
    b_recv,
    r_recv,
    t_recv,
    c_send,
    p_send,
    t_send,
    o_send,
    o_recv,
    load,
):
    tm = lax.axis_index("tm")
    s = lax.axis_index("seq")
    y = tm // 2
    c = tm % 2
    x = s % 4
    image = s // HG
    head0 = (s % HG) * PER
    ypos = y % 4

    loads = [
        pltpu.make_async_copy(src, dst, load.at[n])
        for n, (src, dst) in enumerate(
            [
                (x_hbm, x_ref),
                (mod_hbm, mod_ref),
                (qg_hbm, qg_ref),
                (kg_hbm, kg_ref),
                (mask_hbm, mask_ref),
                (cos_hbm, cos_ref),
                (sin_hbm, sin_ref),
            ]
        )
    ]
    for copy in loads:
        copy.start()

    bar = pltpu.get_barrier_semaphore()

    def greet(i, carry):
        pl.semaphore_signal(bar, inc=1, device_id=(tm, lax.rem(s + i, S)), device_id_type=MESH)
        return carry

    lax.fori_loop(1, S, greet, 0)

    def greet_tm(other):
        pl.semaphore_signal(bar, inc=1, device_id=(other, s), device_id_type=MESH)

    greet_tm(y * 2 + 1 - c)
    zero = jnp.int32(0)

    for sender, receivers in TO.items():
        for receiver in receivers:

            @pl.when(y == receiver)
            def _(sender=sender):
                greet_tm(2 * sender + c)

    loads[0].wait()
    loads[1].wait()
    plan = plan_ref[0]
    stream = jnp.where(s >= TXT // LOC, jnp.int32(1), zero)
    table = mod_ref[plan].astype(F32)
    text = stream == 0
    shift = jnp.where(text, table[0, 0:1], table[0, 1:2])
    scale = 1.0 + jnp.where(text, table[1, 0:1], table[1, 1:2])

    def modulate(b, carry):
        rows = x_ref[b].astype(F32)
        center = jnp.mean(rows, axis=-1, keepdims=True)
        rows = rows - center
        spread = jnp.mean(rows * rows, axis=-1, keepdims=True)
        u = (rows * lax.rsqrt(spread + 1e-06) * scale + shift).astype(BF16)
        for h in range(H):
            send_u[b * HG + h // PER, h % PER] = u[:, h * HD : (h + 1) * HD]
        return carry

    lax.fori_loop(0, B, modulate, 0)

    expected = S - 1 + 1
    for sender, receivers in TO.items():
        expected = expected + jnp.where(y == sender, jnp.int32(len(receivers)), zero)
    pl.semaphore_wait(bar, expected)

    for j in range(PER):
        pltpu.make_async_copy(send_u.at[s, j], recv_u.at[j, s], in_recv.at[j]).start()

        def spread_u(i, carry, j=j):
            p = lax.rem(s + i, S)
            pltpu.make_async_remote_copy(
                send_u.at[p, j],
                recv_u.at[j, s],
                in_send,
                in_recv.at[j],
                device_id=(tm, p),
                device_id_type=MESH,
            ).start()
            return carry

        lax.fori_loop(1, S, spread_u, 0)

    for copy in loads[2:]:
        copy.wait()

    lane = lax.broadcasted_iota(jnp.int32, (L, HD), 1)
    tile = lax.broadcasted_iota(jnp.int32, (L, HD), 0) // 128
    q_aug[:, HD:] = jnp.where(lane == tile, 1.0, 0.0).astype(BF16)
    v_aug[:, HD:] = jnp.ones((L, HD), BF16)
    lane_row = lax.broadcasted_iota(jnp.int32, (HD, HD), 0)
    lane_col = lax.broadcasted_iota(jnp.int32, (HD, HD), 1)
    partner = jnp.where(lane_col % 2 == 0, lane_col + 1, lane_col - 1)
    swap = jnp.where(lane_row == partner, 1.0, 0.0).astype(BF16)
    even = lax.broadcasted_iota(jnp.int32, (8, HD), 1) % 2 == 0
    factor = HD ** (-0.5) * 1.4426950408889634
    step = step_ref[0]

    def swapped(row):
        row = jnp.broadcast_to(row, (8, HD))
        return jnp.where(even, pltpu.roll(row, HD - 1, 1), pltpu.roll(row, 1, 1))[0:1]

    def ex_copy(j):
        return pltpu.make_async_remote_copy(
            ex_out.at[j],
            ex_in.at[j],
            ex_send.at[j],
            ex_recv.at[j],
            device_id=(y * 2 + 1 - c, s),
            device_id_type=MESH,
        )

    def attention(j):
        head = head0 + j
        cols = pl.ds(pl.multiple_of(head * HD, HD), HD)
        pltpu.make_async_copy(recv_u.at[j], recv_u.at[j], in_recv.at[j]).wait()
        u = recv_u[j].reshape(L, HD)
        v_aug[:, :HD] = u
        u32 = u.astype(F32)
        inv = lax.rsqrt(jnp.mean(u32 * u32, axis=-1, keepdims=True) + 1e-06)
        n32 = u32 * inv
        turned = jnp.dot(u[TXT:], swap, preferred_element_type=F32) * inv[TXT:]
        cosine = cos_ref[...]
        sine = sin_ref[...]

        def fill(target, gain_ref, extra):
            gain = gain_ref[:, cols] * extra
            target[:TXT, :HD] = (n32[:TXT] * gain[0:1]).astype(BF16)
            target[TXT:, :HD] = (
                n32[TXT:] * (cosine * gain[1:2]) + turned * (sine * swapped(gain[1:2]))
            ).astype(BF16)

        fill(q_aug, qg_ref, factor)
        fill(k_aug, kg_ref, 1.0)
        masks = mask_ref[...].astype(F32)
        of_head = lax.broadcasted_iota(jnp.int32, masks.shape, 2) == head
        kept = jnp.sum(jnp.where(of_head, masks, 0.0), axis=2, keepdims=True)
        lanes = lax.broadcasted_iota(jnp.int32, (8, HD), 1)
        bias = jnp.zeros((8, HD), F32)
        for a in range(8):
            bias = jnp.where(lanes == a, (1.0 - kept[a]) * NEG, bias)
        for b in range(8):
            k_aug[b * 128 : (b + 1) * 128, HD:] = jnp.broadcast_to(bias[b : b + 1, :], (128, HD)).astype(BF16)

        gates = mod_ref[plan, 2, :, cols].astype(F32) * step
        gate_text, gate_image = gates[0:1], gates[1:2]

        def rows_of(core):
            first = (1 - core) * (TXT // 2)
            text = pl.ds(pl.multiple_of(first, TXT // 2), TXT // 2)
            picture = pl.ds(pl.multiple_of(TXT + first, TXT // 2), TXT // 2)
            query = jnp.concatenate([q_aug[text, :], q_aug[picture, :]], axis=0)
            scores = lax.dot_general(query, k_aug[...], (((1,), (1,)), ((), ())), preferred_element_type=F32)
            top = jnp.max(scores, axis=-1, keepdims=True)
            weights = jnp.exp2(scores - top).astype(BF16)
            summed = jnp.dot(weights, v_aug[...], preferred_element_type=F32)
            result = summed[:, :HD] / summed[:, HD:]
            return result[: TXT // 2] * gate_text, result[TXT // 2 :] * gate_image

        for n, part in enumerate(rows_of(1 - c)):
            ex_out[j, n * (HALF // 2) : (n + 1) * (HALF // 2)] = part.astype(BF16)
        ex_copy(j).start()
        for n, part in enumerate(rows_of(c)):
            own[j, n * (HALF // 2) : (n + 1) * (HALF // 2)] = part

    def chunk_of(i):
        return i // 2 * 2 + lax.rem(i + x, 2)

    def both(j, r):
        mine = own[j, pl.ds(pl.multiple_of(r * CH, CH), CH), :]
        other = ex_in[j, pl.ds(pl.multiple_of(r * CH, CH), CH), :].astype(F32)
        return mine, other

    def hop(src, dst, send_sem, recv_sem, to):
        return pltpu.make_async_remote_copy(src, dst, send_sem, recv_sem, device_id=(to, s), device_id_type=MESH)

    def push_copy(g, dst, recv, to):
        return hop(c_out.at[g], dst.at[g], c_send.at[g], recv.at[g], 2 * to + c)

    def back_copy(g):
        return hop(c_out.at[g], b_in.at[g], p_send.at[0, g], b_recv.at[g], 2 * (y - 1) + c)

    def pair_copy(g, n, dst, recv, to):
        return hop(p_out.at[g], dst.at[g], p_send.at[n, g], recv.at[g], 2 * to + c)

    def total_copy(g, n):
        to = jnp.where(y == 3, 5 - n, 7 - n)
        return hop(t_out.at[g], t_in.at[g], t_send.at[n, g], t_recv.at[g], 2 * to + c)

    def got(recv, g):
        hop(c_out.at[g], a_in.at[g], c_send.at[g], recv.at[g], tm).wait_recv()

    def chunks(j, one_chunk, low=0, high=NCH):
        def run(i, carry):
            r = chunk_of(i)
            one_chunk(r, j * NCH + r)
            return carry

        lax.fori_loop(low, high, run, 0)

    sides = ((0, NCH // 2), (NCH // 2, NCH))

    def push(j):
        ex_copy(j).wait()

        def one_chunk(r, g):
            mine, other = both(j, r)
            c_out[g] = (mine + other).astype(BF16)
            pl.when(ypos == 0)(lambda: push_copy(g, a_in, a_recv, y + 1).start())
            pl.when(y == 2)(lambda: back_copy(g).start())
            pl.when(ypos == 2)(lambda: push_copy(g, b_in, b_recv, y + 1).start())
            pl.when(y == 3)(lambda: push_copy(g, r_in, r_recv, y - 2).start())

        chunks(j, one_chunk)

    def middle_chunk(j):
        def one_chunk(r, g):
            mine, other = both(j, r)
            got(a_recv, g)
            p_out[g] = (mine + other + a_in[g].astype(F32)).astype(BF16)
            pair_copy(g, 0, a_in, a_recv, y + 2).start()

        return one_chunk

    def middle_rest(j, side):
        chunks(j, lambda r, g: pair_copy(g, 1, a_in, a_recv, y + 1).start(), *side)

    def middle(j):
        for side in sides:
            chunks(j, middle_chunk(j), *side)
            middle_rest(j, side)

    def total_chunk(j):
        def one_chunk(r, g):
            mine, other = both(j, r)
            pl.when(y == 3)(lambda: got(a_recv, g))
            got(b_recv, g)
            before = mine + other + a_in[g].astype(F32) + b_in[g].astype(F32)

            @pl.when(y == 3)
            def _():
                t_out[g] = before.astype(BF16)

            @pl.when(y == 1)
            def _():
                got(r_recv, g)
                t_out[g] = (before + r_in[g].astype(F32)).astype(BF16)

            total_copy(g, 0).start()

        return one_chunk

    def total_rest(j, side):
        chunks(j, lambda r, g: total_copy(g, 1).start(), *side)

    def total(j):
        for side in sides:
            chunks(j, total_chunk(j), *side)
            total_rest(j, side)

    def at_once(j, first, k, second, side):
        def run(i, carry):
            r = chunk_of(i)
            first(r, j * NCH + r)
            second(r, k * NCH + r)
            return carry

        lax.fori_loop(side[0], side[1], run, 0)

    def deliver_chunk(j):
        cols = pl.ds(pl.multiple_of((head0 + j) * HD, HD), HD)

        def one_chunk(r, g):
            mine, other = both(j, r)

            def put(before):
                after = before + mine + other
                first = before + jnp.where(c == 0, mine, other)
                d_out[0, g] = first.astype(BF16)
                d_out[1, g] = after.astype(BF16)

            pl.when((ypos == 2) | (y == 7))(lambda: got(a_recv, g))
            pl.when(y == 7)(lambda: got(b_recv, g))
            pl.when(y >= 4)(lambda: got(t_recv, g))

            def put_sum(*refs):
                put(sum(ref[g].astype(F32) for ref in refs))

            pl.when(y == 0)(lambda: put(jnp.zeros((CH, HD), F32)))
            pl.when((y == 1) | (y == 2))(lambda: put_sum(a_in))
            pl.when(y == 3)(lambda: put_sum(a_in, b_in))
            pl.when(y == 4)(lambda: put_sum(t_in))
            pl.when((y == 5) | (y == 6))(lambda: put_sum(t_in, a_in))
            pl.when(y == 7)(lambda: put_sum(t_in, a_in, b_in))

            def piece(i, carry):
                step_to = y * 2 + i // 4
                shard = r // 2 * (S // 2) + (1 - c) * (S // 4) + r % 2 * 4 + lax.rem(i + s // 4, 4)
                src = d_out.at[i // 4, g, pl.ds(pl.multiple_of(lax.rem(i + s // 4, 4) * LOC, LOC), LOC)]
                dst = out_ref.at[image, :, cols]
                here = (shard == s) & (step_to == tm)

                @pl.when(here)
                def _():
                    pltpu.make_async_copy(src, dst, o_recv).start()

                @pl.when(jnp.logical_not(here))
                def _():
                    pltpu.make_async_remote_copy(
                        src, dst, o_send, o_recv, device_id=(step_to, shard), device_id_type=MESH
                    ).start()

                return carry

            lax.fori_loop(0, 8, piece, 0)

        return one_chunk

    def deliver(j):
        chunks(j, deliver_chunk(j))

    attention(0)
    push(0)
    pl.when(y == 1)(lambda: middle(0))
    attention(1)
    push(1)
    pl.when(y == 5)(lambda: middle(0))
    pl.when((y == 1) | (y == 3))(lambda: total(0))
    pl.when((y < 2) | (y == 3))(lambda: deliver(0))
    attention(2)
    pl.when(y == 1)(lambda: middle(1))
    push(2)

    @pl.when(y == 1)
    def _():
        for side in sides:
            at_once(1, total_chunk(1), 2, middle_chunk(2), side)
            total_rest(1, side)
            middle_rest(2, side)

    @pl.when(y == 3)
    def _():
        for j in (1, 2):
            for side in sides:
                at_once(j, total_chunk(j), j, deliver_chunk(j), side)
                total_rest(j, side)

    pl.when((y == 2) | (y >= 4))(lambda: deliver(0))

    @pl.when(y == 5)
    def _():
        middle(1)
        middle(2)

    pl.when(y != 3)(lambda: deliver(1))
    pl.when(y == 1)(lambda: total(2))
    pl.when(y != 3)(lambda: deliver(2))

    sent = send_u.at[pl.ds(0, S - 1)]
    pltpu.make_async_copy(sent, sent, in_send).wait()

    def drain(g, carry):
        pl.when((ypos == 0) | (ypos == 2) | (y == 3))(lambda: push_copy(g, a_in, a_recv, y).wait_send())
        pl.when((ypos == 1) | (y == 2))(lambda: pair_copy(g, 0, a_in, a_recv, y).wait_send())
        pl.when(ypos == 1)(lambda: pair_copy(g, 1, a_in, a_recv, y).wait_send())

        @pl.when((y == 1) | (y == 3))
        def _():
            total_copy(g, 0).wait_send()
            total_copy(g, 1).wait_send()

        return carry

    lax.fori_loop(0, PER * NCH, drain, 0)
    most = d_out.at[0, :, pl.ds(0, CH - LOC)]
    pltpu.make_async_copy(d_out.at[1], d_out.at[1], o_send).wait()
    pltpu.make_async_copy(most, most, o_send).wait()
    rest = d_out.at[0, :, pl.ds(0, LOC)]
    last = d_out.at[0, pl.ds(0, 9), pl.ds(0, LOC)]
    holds_own = 1 - c == s // (S // 4) % 2

    @pl.when(holds_own)
    def _():
        pltpu.make_async_copy(last, last, o_send).wait()

    @pl.when(jnp.logical_not(holds_own))
    def _():
        pltpu.make_async_copy(rest, rest, o_send).wait()

    pltpu.make_async_copy(out_ref, out_ref, o_recv).wait()


def body(trajectory, plan, step_sizes, modulation, q_gain, k_gain, tile_mask):
    cosine, sine = rope_tables()
    n = PER * NCH
    smem = pl.BlockSpec(memory_space=pltpu.SMEM)
    dma = pltpu.SemaphoreType.DMA
    blocks = pl.pallas_call(
        kernel,
        out_shape=jax.ShapeDtypeStruct((B, LOC, D), BF16),
        in_specs=[smem, smem] + [pl.BlockSpec(memory_space=pl.ANY)] * 7,
        out_specs=pl.BlockSpec(memory_space=pl.ANY),
        scratch_shapes=[
            pltpu.VMEM((B, LOC, D), BF16),
            pltpu.VMEM((modulation.shape[0], 3, 2, D), BF16),
            pltpu.VMEM((2, D), F32),
            pltpu.VMEM((2, D), F32),
            pltpu.VMEM((L // 128, L // 128, H), jnp.int32),
            pltpu.VMEM((L - TXT, HD), F32),
            pltpu.VMEM((L - TXT, HD), F32),
            pltpu.VMEM((S, PER, LOC, HD), BF16),
            pltpu.VMEM((PER, S, LOC, HD), BF16),
            pltpu.VMEM((L, 2 * HD), BF16),
            pltpu.VMEM((L, 2 * HD), BF16),
            pltpu.VMEM((L, 2 * HD), BF16),
            pltpu.VMEM((PER, HALF, HD), F32),
            pltpu.VMEM((PER, HALF, HD), BF16),
            pltpu.VMEM((PER, HALF, HD), BF16),
            pltpu.VMEM((n, CH, HD), BF16),
            pltpu.VMEM((n, CH, HD), BF16),
            pltpu.VMEM((n, CH, HD), BF16),
            pltpu.VMEM((n, CH, HD), BF16),
            pltpu.VMEM((n, CH, HD), BF16),
            pltpu.VMEM((n, CH, HD), BF16),
            pltpu.VMEM((n, CH, HD), BF16),
            pltpu.VMEM((2, n, CH, HD), BF16),
            dma,
            dma((PER,)),
            dma((PER,)),
            dma((PER,)),
            dma((n,)),
            dma((n,)),
            dma((n,)),
            dma((n,)),
            dma((n,)),
            dma((2, n)),
            dma((2, n)),
            dma,
            dma,
            dma((7,)),
        ],
        compiler_params=pltpu.CompilerParams(
            collective_id=0, has_side_effects=True, vmem_limit_bytes=56 * 1024 * 1024
        ),
    )(plan, step_sizes, trajectory[0], modulation.transpose(0, 2, 1, 3), q_gain, k_gain, tile_mask.transpose(1, 2, 0), jnp.asarray(cosine), jnp.asarray(sine))
    return blocks.astype(F32)[None]


def solution(mesh):
    placed = (P("tm", None, "seq", None), P("tm"), P("tm"), P(), P(), P(), P())
    return jax.shard_map(
        body, mesh=mesh, in_specs=placed, out_specs=P("tm", None, "seq", None), check_vma=False
    )
```

```python
import jax
import jax.numpy as jnp
import numpy as np
from jax import lax
from jax.experimental import pallas as pl
from jax.experimental.pallas import tpu as pltpu
from jax.sharding import PartitionSpec as P

TXT = 512
IMG_W = 64
MESH = pl.DeviceIdType.MESH
F32 = jnp.float32
BF16 = jnp.bfloat16

B, H, HD, D = 4, 24, 128, 3072
L = 1024
S = 32
LOC = L // S
PER = B * H // S
HG = H // PER
HALF = L // 2
CH = 128
NCH = HALF // CH
NEG = -1e30

TO = {0: (1,), 1: (2, 3, 6, 7), 2: (1, 3), 3: (1, 4, 5), 4: (5,), 5: (6, 7), 6: (7,)}


def rope_tables():
    half = HD // 2
    first = HD // 16
    second = (half - first) // 2
    image = np.arange(L - TXT)
    freqs = (np.float32(10000.0) ** (-(np.arange(second, dtype=np.float32) / np.float32(second)))).astype(np.float32)
    row = (image // IMG_W).astype(np.float32)
    col = (image % IMG_W).astype(np.float32)
    angles = np.concatenate(
        [np.zeros((L - TXT, first), np.float32), row[:, None] * freqs[None], col[:, None] * freqs[None]], axis=1
    ).astype(np.float32)
    cosine = np.repeat(np.cos(angles), 2, axis=1)
    sine = np.repeat(np.sin(angles), 2, axis=1)
    sine[:, 0::2] *= -1.0
    return cosine.astype(np.float32), sine.astype(np.float32)


def kernel(
    plan_ref,
    step_ref,
    x_hbm,
    mod_hbm,
    qg_hbm,
    kg_hbm,
    mask_hbm,
    cos_hbm,
    sin_hbm,
    out_ref,
    x_ref,
    mod_ref,
    qg_ref,
    kg_ref,
    mask_ref,
    cos_ref,
    sin_ref,
    send_u,
    recv_u,
    q_aug,
    k_aug,
    v_aug,
    own,
    ex_out,
    ex_in,
    a_in,
    b_in,
    r_in,
    t_in,
    c_out,
    p_out,
    t_out,
    d_out,
    in_send,
    in_recv,
    ex_send,
    ex_recv,
    a_recv,
    b_recv,
    r_recv,
    t_recv,
    c_send,
    p_send,
    t_send,
    o_send,
    o_recv,
    load,
):
    tm = lax.axis_index("tm")
    s = lax.axis_index("seq")
    y = tm // 2
    c = tm % 2
    x = s % 4
    image = s // HG
    head0 = (s % HG) * PER
    ypos = y % 4

    loads = [
        pltpu.make_async_copy(src, dst, load.at[n])
        for n, (src, dst) in enumerate(
            [
                (x_hbm, x_ref),
                (mod_hbm, mod_ref),
                (qg_hbm, qg_ref),
                (kg_hbm, kg_ref),
                (mask_hbm, mask_ref),
                (cos_hbm, cos_ref),
                (sin_hbm, sin_ref),
            ]
        )
    ]
    for copy in loads:
        copy.start()

    bar = pltpu.get_barrier_semaphore()

    def greet(i, carry):
        pl.semaphore_signal(bar, inc=1, device_id=(tm, lax.rem(s + i, S)), device_id_type=MESH)
        return carry

    lax.fori_loop(1, S, greet, 0)

    def greet_tm(other):
        pl.semaphore_signal(bar, inc=1, device_id=(other, s), device_id_type=MESH)

    greet_tm(y * 2 + 1 - c)
    zero = jnp.int32(0)

    for sender, receivers in TO.items():
        for receiver in receivers:

            @pl.when(y == receiver)
            def _(sender=sender):
                greet_tm(2 * sender + c)

    loads[0].wait()
    loads[1].wait()
    plan = plan_ref[0]
    stream = jnp.where(s >= TXT // LOC, jnp.int32(1), zero)
    table = mod_ref[plan].astype(F32)
    text = stream == 0
    shift = jnp.where(text, table[0, 0:1], table[0, 1:2])
    scale = 1.0 + jnp.where(text, table[1, 0:1], table[1, 1:2])

    def modulate(b, carry):
        rows = x_ref[b].astype(F32)
        center = jnp.mean(rows, axis=-1, keepdims=True)
        rows = rows - center
        spread = jnp.mean(rows * rows, axis=-1, keepdims=True)
        u = (rows * lax.rsqrt(spread + 1e-06) * scale + shift).astype(BF16)
        for h in range(H):
            send_u[b * HG + h // PER, h % PER] = u[:, h * HD : (h + 1) * HD]
        return carry

    lax.fori_loop(0, B, modulate, 0)

    expected = S - 1 + 1
    for sender, receivers in TO.items():
        expected = expected + jnp.where(y == sender, jnp.int32(len(receivers)), zero)
    pl.semaphore_wait(bar, expected)

    for j in range(PER):
        pltpu.make_async_copy(send_u.at[s, j], recv_u.at[j, s], in_recv.at[j]).start()

        def spread_u(i, carry, j=j):
            p = lax.rem(s + i, S)
            pltpu.make_async_remote_copy(
                send_u.at[p, j],
                recv_u.at[j, s],
                in_send,
                in_recv.at[j],
                device_id=(tm, p),
                device_id_type=MESH,
            ).start()
            return carry

        lax.fori_loop(1, S, spread_u, 0)

    for copy in loads[2:]:
        copy.wait()

    lane = lax.broadcasted_iota(jnp.int32, (L, HD), 1)
    tile = lax.broadcasted_iota(jnp.int32, (L, HD), 0) // 128
    q_aug[:, HD:] = jnp.where(lane == tile, 1.0, 0.0).astype(BF16)
    v_aug[:, HD:] = jnp.ones((L, HD), BF16)
    lane_row = lax.broadcasted_iota(jnp.int32, (HD, HD), 0)
    lane_col = lax.broadcasted_iota(jnp.int32, (HD, HD), 1)
    partner = jnp.where(lane_col % 2 == 0, lane_col + 1, lane_col - 1)
    swap = jnp.where(lane_row == partner, 1.0, 0.0).astype(BF16)
    even = lax.broadcasted_iota(jnp.int32, (8, HD), 1) % 2 == 0
    factor = HD ** (-0.5) * 1.4426950408889634
    step = step_ref[0]

    def swapped(row):
        row = jnp.broadcast_to(row, (8, HD))
        return jnp.where(even, pltpu.roll(row, HD - 1, 1), pltpu.roll(row, 1, 1))[0:1]

    def ex_copy(j):
        return pltpu.make_async_remote_copy(
            ex_out.at[j],
            ex_in.at[j],
            ex_send.at[j],
            ex_recv.at[j],
            device_id=(y * 2 + 1 - c, s),
            device_id_type=MESH,
        )

    def attention(j):
        head = head0 + j
        cols = pl.ds(pl.multiple_of(head * HD, HD), HD)
        pltpu.make_async_copy(recv_u.at[j], recv_u.at[j], in_recv.at[j]).wait()
        u = recv_u[j].reshape(L, HD)
        v_aug[:, :HD] = u
        u32 = u.astype(F32)
        inv = lax.rsqrt(jnp.mean(u32 * u32, axis=-1, keepdims=True) + 1e-06)
        n32 = u32 * inv
        turned = jnp.dot(u[TXT:], swap, preferred_element_type=F32) * inv[TXT:]
        cosine = cos_ref[...]
        sine = sin_ref[...]

        def fill(target, gain_ref, extra):
            gain = gain_ref[:, cols] * extra
            target[:TXT, :HD] = (n32[:TXT] * gain[0:1]).astype(BF16)
            target[TXT:, :HD] = (
                n32[TXT:] * (cosine * gain[1:2]) + turned * (sine * swapped(gain[1:2]))
            ).astype(BF16)

        fill(q_aug, qg_ref, factor)
        fill(k_aug, kg_ref, 1.0)
        masks = mask_ref[...].astype(F32)
        of_head = lax.broadcasted_iota(jnp.int32, masks.shape, 2) == head
        kept = jnp.sum(jnp.where(of_head, masks, 0.0), axis=2, keepdims=True)
        lanes = lax.broadcasted_iota(jnp.int32, (8, HD), 1)
        bias = jnp.zeros((8, HD), F32)
        for a in range(8):
            bias = jnp.where(lanes == a, (1.0 - kept[a]) * NEG, bias)
        for b in range(8):
            k_aug[b * 128 : (b + 1) * 128, HD:] = jnp.broadcast_to(bias[b : b + 1, :], (128, HD)).astype(BF16)

        gates = mod_ref[plan, 2, :, cols].astype(F32) * step
        gate_text, gate_image = gates[0:1], gates[1:2]

        def rows_of(core):
            first = (1 - core) * (TXT // 2)
            text = pl.ds(pl.multiple_of(first, TXT // 2), TXT // 2)
            picture = pl.ds(pl.multiple_of(TXT + first, TXT // 2), TXT // 2)
            query = jnp.concatenate([q_aug[text, :], q_aug[picture, :]], axis=0)
            scores = lax.dot_general(query, k_aug[...], (((1,), (1,)), ((), ())), preferred_element_type=F32)
            top = jnp.max(scores, axis=-1, keepdims=True)
            weights = jnp.exp2(scores - top).astype(BF16)
            summed = jnp.dot(weights, v_aug[...], preferred_element_type=F32)
            result = summed[:, :HD] / summed[:, HD:]
            return result[: TXT // 2] * gate_text, result[TXT // 2 :] * gate_image

        for n, part in enumerate(rows_of(1 - c)):
            ex_out[j, n * (HALF // 2) : (n + 1) * (HALF // 2)] = part.astype(BF16)
        ex_copy(j).start()
        for n, part in enumerate(rows_of(c)):
            own[j, n * (HALF // 2) : (n + 1) * (HALF // 2)] = part

    def chunk_of(i):
        return i // 2 * 2 + lax.rem(i + x, 2)

    def both(j, r):
        mine = own[j, pl.ds(pl.multiple_of(r * CH, CH), CH), :]
        other = ex_in[j, pl.ds(pl.multiple_of(r * CH, CH), CH), :].astype(F32)
        return mine, other

    def hop(src, dst, send_sem, recv_sem, to):
        return pltpu.make_async_remote_copy(src, dst, send_sem, recv_sem, device_id=(to, s), device_id_type=MESH)

    def push_copy(g, dst, recv, to):
        return hop(c_out.at[g], dst.at[g], c_send.at[g], recv.at[g], 2 * to + c)

    def back_copy(g):
        return hop(c_out.at[g], b_in.at[g], p_send.at[0, g], b_recv.at[g], 2 * (y - 1) + c)

    def pair_copy(g, n, dst, recv, to):
        return hop(p_out.at[g], dst.at[g], p_send.at[n, g], recv.at[g], 2 * to + c)

    def total_copy(g, n):
        to = jnp.where(y == 3, 5 - n, 7 - n)
        return hop(t_out.at[g], t_in.at[g], t_send.at[n, g], t_recv.at[g], 2 * to + c)

    def got(recv, g):
        hop(c_out.at[g], a_in.at[g], c_send.at[g], recv.at[g], tm).wait_recv()

    def chunks(j, one_chunk, low=0, high=NCH):
        def run(i, carry):
            r = chunk_of(i)
            one_chunk(r, j * NCH + r)
            return carry

        lax.fori_loop(low, high, run, 0)

    sides = ((0, NCH // 2), (NCH // 2, NCH))

    def push(j):
        ex_copy(j).wait()

        def one_chunk(r, g):
            mine, other = both(j, r)
            c_out[g] = (mine + other).astype(BF16)
            pl.when(ypos == 0)(lambda: push_copy(g, a_in, a_recv, y + 1).start())
            pl.when(y == 2)(lambda: back_copy(g).start())
            pl.when(ypos == 2)(lambda: push_copy(g, b_in, b_recv, y + 1).start())
            pl.when(y == 3)(lambda: push_copy(g, r_in, r_recv, y - 2).start())

        chunks(j, one_chunk)

    def middle_chunk(j):
        def one_chunk(r, g):
            mine, other = both(j, r)
            got(a_recv, g)
            p_out[g] = (mine + other + a_in[g].astype(F32)).astype(BF16)
            pair_copy(g, 0, a_in, a_recv, y + 2).start()

        return one_chunk

    def middle_rest(j, side):
        chunks(j, lambda r, g: pair_copy(g, 1, a_in, a_recv, y + 1).start(), *side)

    def middle(j):
        for side in sides:
            chunks(j, middle_chunk(j), *side)
            middle_rest(j, side)

    def total_chunk(j):
        def one_chunk(r, g):
            mine, other = both(j, r)
            pl.when(y == 3)(lambda: got(a_recv, g))
            got(b_recv, g)
            before = mine + other + a_in[g].astype(F32) + b_in[g].astype(F32)

            @pl.when(y == 3)
            def _():
                t_out[g] = before.astype(BF16)

            @pl.when(y == 1)
            def _():
                got(r_recv, g)
                t_out[g] = (before + r_in[g].astype(F32)).astype(BF16)

            total_copy(g, 0).start()
            total_copy(g, 1).start()

        return one_chunk

    def total(j):
        for side in sides:
            chunks(j, total_chunk(j), *side)

    def at_once(j, first, k, second, side):
        def run(i, carry):
            r = chunk_of(i)
            first(r, j * NCH + r)
            second(r, k * NCH + r)
            return carry

        lax.fori_loop(side[0], side[1], run, 0)

    def deliver_chunk(j):
        cols = pl.ds(pl.multiple_of((head0 + j) * HD, HD), HD)

        def one_chunk(r, g):
            mine, other = both(j, r)

            def put(before):
                after = before + mine + other
                first = before + jnp.where(c == 0, mine, other)
                d_out[0, g] = first.astype(BF16)
                d_out[1, g] = after.astype(BF16)

            pl.when((ypos == 2) | (y == 7))(lambda: got(a_recv, g))
            pl.when(y == 7)(lambda: got(b_recv, g))
            pl.when(y >= 4)(lambda: got(t_recv, g))

            def put_sum(*refs):
                put(sum(ref[g].astype(F32) for ref in refs))

            pl.when(y == 0)(lambda: put(jnp.zeros((CH, HD), F32)))
            pl.when((y == 1) | (y == 2))(lambda: put_sum(a_in))
            pl.when(y == 3)(lambda: put_sum(a_in, b_in))
            pl.when(y == 4)(lambda: put_sum(t_in))
            pl.when((y == 5) | (y == 6))(lambda: put_sum(t_in, a_in))
            pl.when(y == 7)(lambda: put_sum(t_in, a_in, b_in))

            def piece(i, carry):
                step_to = y * 2 + i // 4
                shard = r // 2 * (S // 2) + (1 - c) * (S // 4) + r % 2 * 4 + lax.rem(i + s // 4, 4)
                src = d_out.at[i // 4, g, pl.ds(pl.multiple_of(lax.rem(i + s // 4, 4) * LOC, LOC), LOC)]
                dst = out_ref.at[image, :, cols]
                here = (shard == s) & (step_to == tm)

                @pl.when(here)
                def _():
                    pltpu.make_async_copy(src, dst, o_recv).start()

                @pl.when(jnp.logical_not(here))
                def _():
                    pltpu.make_async_remote_copy(
                        src, dst, o_send, o_recv, device_id=(step_to, shard), device_id_type=MESH
                    ).start()

                return carry

            lax.fori_loop(0, 8, piece, 0)

        return one_chunk

    def deliver(j):
        chunks(j, deliver_chunk(j))

    attention(0)
    push(0)
    pl.when(y == 1)(lambda: middle(0))
    attention(1)
    pl.when(y == 3)(lambda: total(0))
    push(1)
    pl.when(y == 5)(lambda: middle(0))
    pl.when(y == 1)(lambda: total(0))
    pl.when((y == 0) | (y == 1) | (y == 2) | (y == 3))(lambda: deliver(0))
    attention(2)
    pl.when((y == 4) | (y == 5) | (y == 6) | (y == 7))(lambda: deliver(0))
    pl.when(y == 1)(lambda: middle(1))
    push(2)

    @pl.when(y == 1)
    def _():
        for side in sides:
            at_once(1, total_chunk(1), 2, middle_chunk(2), side)
            middle_rest(2, side)

    @pl.when(y == 3)
    def _():
        for j in (1, 2):
            for side in sides:
                at_once(j, total_chunk(j), j, deliver_chunk(j), side)


    @pl.when(y == 5)
    def _():
        middle(1)
        middle(2)

    pl.when(y != 3)(lambda: deliver(1))
    pl.when(y == 1)(lambda: total(2))
    pl.when(y != 3)(lambda: deliver(2))

    sent = send_u.at[pl.ds(0, S - 1)]
    pltpu.make_async_copy(sent, sent, in_send).wait()

    def drain(g, carry):
        pl.when((ypos == 0) | (ypos == 2) | (y == 3))(lambda: push_copy(g, a_in, a_recv, y).wait_send())
        pl.when((ypos == 1) | (y == 2))(lambda: pair_copy(g, 0, a_in, a_recv, y).wait_send())
        pl.when(ypos == 1)(lambda: pair_copy(g, 1, a_in, a_recv, y).wait_send())

        @pl.when((y == 1) | (y == 3))
        def _():
            total_copy(g, 0).wait_send()
            total_copy(g, 1).wait_send()

        return carry

    lax.fori_loop(0, PER * NCH, drain, 0)
    most = d_out.at[0, :, pl.ds(0, CH - LOC)]
    pltpu.make_async_copy(d_out.at[1], d_out.at[1], o_send).wait()
    pltpu.make_async_copy(most, most, o_send).wait()
    rest = d_out.at[0, :, pl.ds(0, LOC)]
    last = d_out.at[0, pl.ds(0, 9), pl.ds(0, LOC)]
    holds_own = 1 - c == s // (S // 4) % 2

    @pl.when(holds_own)
    def _():
        pltpu.make_async_copy(last, last, o_send).wait()

    @pl.when(jnp.logical_not(holds_own))
    def _():
        pltpu.make_async_copy(rest, rest, o_send).wait()

    pltpu.make_async_copy(out_ref, out_ref, o_recv).wait()


def body(trajectory, plan, step_sizes, modulation, q_gain, k_gain, tile_mask):
    cosine, sine = rope_tables()
    n = PER * NCH
    smem = pl.BlockSpec(memory_space=pltpu.SMEM)
    dma = pltpu.SemaphoreType.DMA
    blocks = pl.pallas_call(
        kernel,
        out_shape=jax.ShapeDtypeStruct((B, LOC, D), BF16),
        in_specs=[smem, smem] + [pl.BlockSpec(memory_space=pl.ANY)] * 7,
        out_specs=pl.BlockSpec(memory_space=pl.ANY),
        scratch_shapes=[
            pltpu.VMEM((B, LOC, D), BF16),
            pltpu.VMEM((modulation.shape[0], 3, 2, D), BF16),
            pltpu.VMEM((2, D), F32),
            pltpu.VMEM((2, D), F32),
            pltpu.VMEM((L // 128, L // 128, H), jnp.int32),
            pltpu.VMEM((L - TXT, HD), F32),
            pltpu.VMEM((L - TXT, HD), F32),
            pltpu.VMEM((S, PER, LOC, HD), BF16),
            pltpu.VMEM((PER, S, LOC, HD), BF16),
            pltpu.VMEM((L, 2 * HD), BF16),
            pltpu.VMEM((L, 2 * HD), BF16),
            pltpu.VMEM((L, 2 * HD), BF16),
            pltpu.VMEM((PER, HALF, HD), F32),
            pltpu.VMEM((PER, HALF, HD), BF16),
            pltpu.VMEM((PER, HALF, HD), BF16),
            pltpu.VMEM((n, CH, HD), BF16),
            pltpu.VMEM((n, CH, HD), BF16),
            pltpu.VMEM((n, CH, HD), BF16),
            pltpu.VMEM((n, CH, HD), BF16),
            pltpu.VMEM((n, CH, HD), BF16),
            pltpu.VMEM((n, CH, HD), BF16),
            pltpu.VMEM((n, CH, HD), BF16),
            pltpu.VMEM((2, n, CH, HD), BF16),
            dma,
            dma((PER,)),
            dma((PER,)),
            dma((PER,)),
            dma((n,)),
            dma((n,)),
            dma((n,)),
            dma((n,)),
            dma((n,)),
            dma((2, n)),
            dma((2, n)),
            dma,
            dma,
            dma((7,)),
        ],
        compiler_params=pltpu.CompilerParams(
            collective_id=0, has_side_effects=True, vmem_limit_bytes=56 * 1024 * 1024
        ),
    )(plan, step_sizes, trajectory[0], modulation.transpose(0, 2, 1, 3), q_gain, k_gain, tile_mask.transpose(1, 2, 0), jnp.asarray(cosine), jnp.asarray(sine))
    return blocks.astype(F32)[None]


def solution(mesh):
    placed = (P("tm", None, "seq", None), P("tm"), P("tm"), P(), P(), P(), P())
    return jax.shard_map(
        body, mesh=mesh, in_specs=placed, out_specs=P("tm", None, "seq", None), check_vma=False
    )
```

```python
import jax
import jax.numpy as jnp
import numpy as np
from jax import lax
from jax.experimental import pallas as pl
from jax.experimental.pallas import tpu as pltpu
from jax.sharding import PartitionSpec as P

TXT = 512
IMG_W = 64
MESH = pl.DeviceIdType.MESH
F32 = jnp.float32
BF16 = jnp.bfloat16

B, H, HD, D = 4, 24, 128, 3072
L = 1024
S = 32
LOC = L // S
PER = B * H // S
HG = H // PER
HALF = L // 2
CH = 128
NCH = HALF // CH
NEG = -1e30

TO = {0: (1,), 1: (2, 3, 6, 7), 2: (1, 3), 3: (1, 4, 5), 4: (5,), 5: (6, 7), 6: (7,)}


def rope_tables():
    half = HD // 2
    first = HD // 16
    second = (half - first) // 2
    image = np.arange(L - TXT)
    freqs = (np.float32(10000.0) ** (-(np.arange(second, dtype=np.float32) / np.float32(second)))).astype(np.float32)
    row = (image // IMG_W).astype(np.float32)
    col = (image % IMG_W).astype(np.float32)
    angles = np.concatenate(
        [np.zeros((L - TXT, first), np.float32), row[:, None] * freqs[None], col[:, None] * freqs[None]], axis=1
    ).astype(np.float32)
    cosine = np.repeat(np.cos(angles), 2, axis=1)
    sine = np.repeat(np.sin(angles), 2, axis=1)
    sine[:, 0::2] *= -1.0
    return cosine.astype(np.float32), sine.astype(np.float32)


def kernel(
    plan_ref,
    step_ref,
    x_hbm,
    mod_hbm,
    qg_hbm,
    kg_hbm,
    mask_hbm,
    cos_hbm,
    sin_hbm,
    out_ref,
    x_ref,
    mod_ref,
    qg_ref,
    kg_ref,
    mask_ref,
    cos_ref,
    sin_ref,
    send_u,
    recv_u,
    q_aug,
    k_aug,
    v_aug,
    own,
    ex_out,
    ex_in,
    a_in,
    b_in,
    r_in,
    t_in,
    c_out,
    p_out,
    t_out,
    d_out,
    in_send,
    in_recv,
    ex_send,
    ex_recv,
    a_recv,
    b_recv,
    r_recv,
    t_recv,
    c_send,
    p_send,
    t_send,
    o_send,
    o_recv,
    load,
):
    tm = lax.axis_index("tm")
    s = lax.axis_index("seq")
    y = tm // 2
    c = tm % 2
    x = s % 4
    image = s // HG
    head0 = (s % HG) * PER
    ypos = y % 4

    loads = [
        pltpu.make_async_copy(src, dst, load.at[n])
        for n, (src, dst) in enumerate(
            [
                (x_hbm, x_ref),
                (mod_hbm, mod_ref),
                (qg_hbm, qg_ref),
                (kg_hbm, kg_ref),
                (mask_hbm, mask_ref),
                (cos_hbm, cos_ref),
                (sin_hbm, sin_ref),
            ]
        )
    ]
    for copy in loads:
        copy.start()

    bar = pltpu.get_barrier_semaphore()

    def greet(i, carry):
        pl.semaphore_signal(bar, inc=1, device_id=(tm, lax.rem(s + i, S)), device_id_type=MESH)
        return carry

    lax.fori_loop(1, S, greet, 0)

    def greet_tm(other):
        pl.semaphore_signal(bar, inc=1, device_id=(other, s), device_id_type=MESH)

    greet_tm(y * 2 + 1 - c)
    zero = jnp.int32(0)

    for sender, receivers in TO.items():
        for receiver in receivers:

            @pl.when(y == receiver)
            def _(sender=sender):
                greet_tm(2 * sender + c)

    loads[0].wait()
    loads[1].wait()
    plan = plan_ref[0]
    stream = jnp.where(s >= TXT // LOC, jnp.int32(1), zero)
    table = mod_ref[plan].astype(F32)
    text = stream == 0
    shift = jnp.where(text, table[0, 0:1], table[0, 1:2])
    scale = 1.0 + jnp.where(text, table[1, 0:1], table[1, 1:2])

    def modulate(b, carry):
        rows = x_ref[b].astype(F32)
        center = jnp.mean(rows, axis=-1, keepdims=True)
        rows = rows - center
        spread = jnp.mean(rows * rows, axis=-1, keepdims=True)
        u = (rows * lax.rsqrt(spread + 1e-06) * scale + shift).astype(BF16)
        for h in range(H):
            send_u[b * HG + h // PER, h % PER] = u[:, h * HD : (h + 1) * HD]
        return carry

    lax.fori_loop(0, B, modulate, 0)

    expected = S - 1 + 1
    for sender, receivers in TO.items():
        expected = expected + jnp.where(y == sender, jnp.int32(len(receivers)), zero)
    pl.semaphore_wait(bar, expected)

    for j in range(PER):
        pltpu.make_async_copy(send_u.at[s, j], recv_u.at[j, s], in_recv.at[j]).start()

        def spread_u(i, carry, j=j):
            p = lax.rem(s + i, S)
            pltpu.make_async_remote_copy(
                send_u.at[p, j],
                recv_u.at[j, s],
                in_send,
                in_recv.at[j],
                device_id=(tm, p),
                device_id_type=MESH,
            ).start()
            return carry

        lax.fori_loop(1, S, spread_u, 0)

    for copy in loads[2:]:
        copy.wait()

    lane = lax.broadcasted_iota(jnp.int32, (L, HD), 1)
    tile = lax.broadcasted_iota(jnp.int32, (L, HD), 0) // 128
    q_aug[:, HD:] = jnp.where(lane == tile, 1.0, 0.0).astype(BF16)
    v_aug[:, HD:] = jnp.ones((L, HD), BF16)
    lane_row = lax.broadcasted_iota(jnp.int32, (HD, HD), 0)
    lane_col = lax.broadcasted_iota(jnp.int32, (HD, HD), 1)
    partner = jnp.where(lane_col % 2 == 0, lane_col + 1, lane_col - 1)
    swap = jnp.where(lane_row == partner, 1.0, 0.0).astype(BF16)
    even = lax.broadcasted_iota(jnp.int32, (8, HD), 1) % 2 == 0
    factor = HD ** (-0.5) * 1.4426950408889634
    step = step_ref[0]

    def swapped(row):
        row = jnp.broadcast_to(row, (8, HD))
        return jnp.where(even, pltpu.roll(row, HD - 1, 1), pltpu.roll(row, 1, 1))[0:1]

    def ex_copy(j):
        return pltpu.make_async_remote_copy(
            ex_out.at[j],
            ex_in.at[j],
            ex_send.at[j],
            ex_recv.at[j],
            device_id=(y * 2 + 1 - c, s),
            device_id_type=MESH,
        )

    def attention(j):
        head = head0 + j
        cols = pl.ds(pl.multiple_of(head * HD, HD), HD)
        pltpu.make_async_copy(recv_u.at[j], recv_u.at[j], in_recv.at[j]).wait()
        u = recv_u[j].reshape(L, HD)
        v_aug[:, :HD] = u
        u32 = u.astype(F32)
        inv = lax.rsqrt(jnp.mean(u32 * u32, axis=-1, keepdims=True) + 1e-06)
        n32 = u32 * inv
        turned = jnp.dot(u[TXT:], swap, preferred_element_type=F32) * inv[TXT:]
        cosine = cos_ref[...]
        sine = sin_ref[...]

        def fill(target, gain_ref, extra):
            gain = gain_ref[:, cols] * extra
            target[:TXT, :HD] = (n32[:TXT] * gain[0:1]).astype(BF16)
            target[TXT:, :HD] = (
                n32[TXT:] * (cosine * gain[1:2]) + turned * (sine * swapped(gain[1:2]))
            ).astype(BF16)

        fill(q_aug, qg_ref, factor)
        fill(k_aug, kg_ref, 1.0)
        masks = mask_ref[...].astype(F32)
        of_head = lax.broadcasted_iota(jnp.int32, masks.shape, 2) == head
        kept = jnp.sum(jnp.where(of_head, masks, 0.0), axis=2, keepdims=True)
        lanes = lax.broadcasted_iota(jnp.int32, (8, HD), 1)
        bias = jnp.zeros((8, HD), F32)
        for a in range(8):
            bias = jnp.where(lanes == a, (1.0 - kept[a]) * NEG, bias)
        for b in range(8):
            k_aug[b * 128 : (b + 1) * 128, HD:] = jnp.broadcast_to(bias[b : b + 1, :], (128, HD)).astype(BF16)

        gates = mod_ref[plan, 2, :, cols].astype(F32) * step
        gate_text, gate_image = gates[0:1], gates[1:2]

        def rows_of(core):
            first = (1 - core) * (TXT // 2)
            text = pl.ds(pl.multiple_of(first, TXT // 2), TXT // 2)
            picture = pl.ds(pl.multiple_of(TXT + first, TXT // 2), TXT // 2)
            query = jnp.concatenate([q_aug[text, :], q_aug[picture, :]], axis=0)
            scores = lax.dot_general(query, k_aug[...], (((1,), (1,)), ((), ())), preferred_element_type=F32)
            top = jnp.max(scores, axis=-1, keepdims=True)
            weights = jnp.exp2(scores - top).astype(BF16)
            summed = jnp.dot(weights, v_aug[...], preferred_element_type=F32)
            result = summed[:, :HD] / summed[:, HD:]
            return result[: TXT // 2] * gate_text, result[TXT // 2 :] * gate_image

        for n, part in enumerate(rows_of(1 - c)):
            ex_out[j, n * (HALF // 2) : (n + 1) * (HALF // 2)] = part.astype(BF16)
        ex_copy(j).start()
        for n, part in enumerate(rows_of(c)):
            own[j, n * (HALF // 2) : (n + 1) * (HALF // 2)] = part

    def chunk_of(i):
        return i // 2 * 2 + lax.rem(i + x, 2)

    def both(j, r):
        mine = own[j, pl.ds(pl.multiple_of(r * CH, CH), CH), :]
        other = ex_in[j, pl.ds(pl.multiple_of(r * CH, CH), CH), :].astype(F32)
        return mine, other

    def hop(src, dst, send_sem, recv_sem, to):
        return pltpu.make_async_remote_copy(src, dst, send_sem, recv_sem, device_id=(to, s), device_id_type=MESH)

    def push_copy(g, dst, recv, to):
        return hop(c_out.at[g], dst.at[g], c_send.at[g], recv.at[g], 2 * to + c)

    def back_copy(g):
        return hop(c_out.at[g], b_in.at[g], p_send.at[0, g], b_recv.at[g], 2 * (y - 1) + c)

    def pair_copy(g, n, dst, recv, to):
        return hop(p_out.at[g], dst.at[g], p_send.at[n, g], recv.at[g], 2 * to + c)

    def total_copy(g, n):
        to = jnp.where(y == 3, 5 - n, 7 - n)
        return hop(t_out.at[g], t_in.at[g], t_send.at[n, g], t_recv.at[g], 2 * to + c)

    def got(recv, g):
        hop(c_out.at[g], a_in.at[g], c_send.at[g], recv.at[g], tm).wait_recv()

    def chunks(j, one_chunk, low=0, high=NCH):
        def run(i, carry):
            r = chunk_of(i)
            one_chunk(r, j * NCH + r)
            return carry

        lax.fori_loop(low, high, run, 0)

    sides = ((0, NCH // 2), (NCH // 2, NCH))

    def push(j):
        ex_copy(j).wait()

        def one_chunk(r, g):
            mine, other = both(j, r)
            c_out[g] = (mine + other).astype(BF16)
            pl.when(ypos == 0)(lambda: push_copy(g, a_in, a_recv, y + 1).start())
            pl.when(y == 2)(lambda: back_copy(g).start())
            pl.when(ypos == 2)(lambda: push_copy(g, b_in, b_recv, y + 1).start())
            pl.when(y == 3)(lambda: push_copy(g, r_in, r_recv, y - 2).start())

        chunks(j, one_chunk)

    def middle_chunk(j):
        def one_chunk(r, g):
            mine, other = both(j, r)
            got(a_recv, g)
            p_out[g] = (mine + other + a_in[g].astype(F32)).astype(BF16)
            pair_copy(g, 0, a_in, a_recv, y + 2).start()

        return one_chunk

    def middle_rest(j, side):
        chunks(j, lambda r, g: pair_copy(g, 1, a_in, a_recv, y + 1).start(), *side)

    def middle(j):
        for side in sides:
            chunks(j, middle_chunk(j), *side)
            middle_rest(j, side)

    def total_chunk(j):
        def one_chunk(r, g):
            mine, other = both(j, r)
            pl.when(y == 3)(lambda: got(a_recv, g))
            got(b_recv, g)
            before = mine + other + a_in[g].astype(F32) + b_in[g].astype(F32)

            @pl.when(y == 3)
            def _():
                t_out[g] = before.astype(BF16)

            @pl.when(y == 1)
            def _():
                got(r_recv, g)
                t_out[g] = (before + r_in[g].astype(F32)).astype(BF16)

            total_copy(g, 0).start()
            total_copy(g, 1).start()

        return one_chunk

    def total(j):
        for side in sides:
            chunks(j, total_chunk(j), *side)

    def at_once(j, first, k, second, side):
        def run(i, carry):
            r = chunk_of(i)
            first(r, j * NCH + r)
            second(r, k * NCH + r)
            return carry

        lax.fori_loop(side[0], side[1], run, 0)

    def deliver_chunk(j):
        cols = pl.ds(pl.multiple_of((head0 + j) * HD, HD), HD)

        def one_chunk(r, g):
            mine, other = both(j, r)

            def put(before):
                after = before + mine + other
                first = before + jnp.where(c == 0, mine, other)
                d_out[0, g] = first.astype(BF16)
                d_out[1, g] = after.astype(BF16)

            pl.when((ypos == 2) | (y == 7))(lambda: got(a_recv, g))
            pl.when(y == 7)(lambda: got(b_recv, g))
            pl.when(y >= 4)(lambda: got(t_recv, g))

            def put_sum(*refs):
                put(sum(ref[g].astype(F32) for ref in refs))

            pl.when(y == 0)(lambda: put(jnp.zeros((CH, HD), F32)))
            pl.when((y == 1) | (y == 2))(lambda: put_sum(a_in))
            pl.when(y == 3)(lambda: put_sum(a_in, b_in))
            pl.when(y == 4)(lambda: put_sum(t_in))
            pl.when((y == 5) | (y == 6))(lambda: put_sum(t_in, a_in))
            pl.when(y == 7)(lambda: put_sum(t_in, a_in, b_in))

            def piece(i, carry):
                step_to = y * 2 + i // 4
                shard = r // 2 * (S // 2) + (1 - c) * (S // 4) + r % 2 * 4 + lax.rem(i + s // 4, 4)
                src = d_out.at[i // 4, g, pl.ds(pl.multiple_of(lax.rem(i + s // 4, 4) * LOC, LOC), LOC)]
                dst = out_ref.at[image, :, cols]
                here = (shard == s) & (step_to == tm)

                @pl.when(here)
                def _():
                    pltpu.make_async_copy(src, dst, o_recv).start()

                @pl.when(jnp.logical_not(here))
                def _():
                    pltpu.make_async_remote_copy(
                        src, dst, o_send, o_recv, device_id=(step_to, shard), device_id_type=MESH
                    ).start()

                return carry

            lax.fori_loop(0, 8, piece, 0)

        return one_chunk

    def deliver(j):
        chunks(j, deliver_chunk(j))

    attention(0)
    push(0)
    pl.when(y == 1)(lambda: middle(0))
    attention(1)
    pl.when(y == 3)(lambda: total(0))
    push(1)
    pl.when(y == 5)(lambda: middle(0))
    pl.when(y == 1)(lambda: total(0))
    pl.when((y == 0) | (y == 1) | (y == 2) | (y == 3))(lambda: deliver(0))
    attention(2)
    pl.when((y == 4) | (y == 5) | (y == 6) | (y == 7))(lambda: deliver(0))
    pl.when(y == 1)(lambda: middle(1))
    push(2)

    @pl.when(y == 1)
    def _():
        for side in sides:
            at_once(1, total_chunk(1), 2, middle_chunk(2), side)
            middle_rest(2, side)

    @pl.when(y == 3)
    def _():
        for j in (1, 2):
            for side in sides:
                at_once(j, total_chunk(j), j, deliver_chunk(j), side)


    @pl.when(y == 5)
    def _():
        middle(1)
        for side in sides:
            at_once(2, middle_chunk(2), 1, deliver_chunk(1), side)
            middle_rest(2, side)

    pl.when((y != 3) & (y != 5))(lambda: deliver(1))
    pl.when(y == 1)(lambda: total(2))
    pl.when(y != 3)(lambda: deliver(2))

    sent = send_u.at[pl.ds(0, S - 1)]
    pltpu.make_async_copy(sent, sent, in_send).wait()

    def drain(g, carry):
        pl.when((ypos == 0) | (ypos == 2) | (y == 3))(lambda: push_copy(g, a_in, a_recv, y).wait_send())
        pl.when((ypos == 1) | (y == 2))(lambda: pair_copy(g, 0, a_in, a_recv, y).wait_send())
        pl.when(ypos == 1)(lambda: pair_copy(g, 1, a_in, a_recv, y).wait_send())

        @pl.when((y == 1) | (y == 3))
        def _():
            total_copy(g, 0).wait_send()
            total_copy(g, 1).wait_send()

        return carry

    lax.fori_loop(0, PER * NCH, drain, 0)
    most = d_out.at[0, :, pl.ds(0, CH - LOC)]
    pltpu.make_async_copy(d_out.at[1], d_out.at[1], o_send).wait()
    pltpu.make_async_copy(most, most, o_send).wait()
    rest = d_out.at[0, :, pl.ds(0, LOC)]
    last = d_out.at[0, pl.ds(0, 9), pl.ds(0, LOC)]
    holds_own = 1 - c == s // (S // 4) % 2

    @pl.when(holds_own)
    def _():
        pltpu.make_async_copy(last, last, o_send).wait()

    @pl.when(jnp.logical_not(holds_own))
    def _():
        pltpu.make_async_copy(rest, rest, o_send).wait()

    pltpu.make_async_copy(out_ref, out_ref, o_recv).wait()


def widen(src, dst, narrow, wide, read, write):
    ins = [pltpu.make_async_copy(src.at[b], narrow.at[b], read.at[b]) for b in range(B)]
    outs = [pltpu.make_async_copy(wide.at[b], dst.at[b], write.at[b]) for b in range(B)]
    for copy in ins:
        copy.start()
    for b in range(B):
        ins[b].wait()
        wide[b] = narrow[b].astype(F32)
        outs[b].start()
    for copy in outs:
        copy.wait()


def body(trajectory, plan, step_sizes, modulation, q_gain, k_gain, tile_mask):
    cosine, sine = rope_tables()
    n = PER * NCH
    smem = pl.BlockSpec(memory_space=pltpu.SMEM)
    dma = pltpu.SemaphoreType.DMA
    blocks = pl.pallas_call(
        kernel,
        out_shape=jax.ShapeDtypeStruct((B, LOC, D), BF16),
        in_specs=[smem, smem] + [pl.BlockSpec(memory_space=pl.ANY)] * 7,
        out_specs=pl.BlockSpec(memory_space=pl.ANY),
        scratch_shapes=[
            pltpu.VMEM((B, LOC, D), BF16),
            pltpu.VMEM((modulation.shape[0], 3, 2, D), BF16),
            pltpu.VMEM((2, D), F32),
            pltpu.VMEM((2, D), F32),
            pltpu.VMEM((L // 128, L // 128, H), jnp.int32),
            pltpu.VMEM((L - TXT, HD), F32),
            pltpu.VMEM((L - TXT, HD), F32),
            pltpu.VMEM((S, PER, LOC, HD), BF16),
            pltpu.VMEM((PER, S, LOC, HD), BF16),
            pltpu.VMEM((L, 2 * HD), BF16),
            pltpu.VMEM((L, 2 * HD), BF16),
            pltpu.VMEM((L, 2 * HD), BF16),
            pltpu.VMEM((PER, HALF, HD), F32),
            pltpu.VMEM((PER, HALF, HD), BF16),
            pltpu.VMEM((PER, HALF, HD), BF16),
            pltpu.VMEM((n, CH, HD), BF16),
            pltpu.VMEM((n, CH, HD), BF16),
            pltpu.VMEM((n, CH, HD), BF16),
            pltpu.VMEM((n, CH, HD), BF16),
            pltpu.VMEM((n, CH, HD), BF16),
            pltpu.VMEM((n, CH, HD), BF16),
            pltpu.VMEM((n, CH, HD), BF16),
            pltpu.VMEM((2, n, CH, HD), BF16),
            dma,
            dma((PER,)),
            dma((PER,)),
            dma((PER,)),
            dma((n,)),
            dma((n,)),
            dma((n,)),
            dma((n,)),
            dma((n,)),
            dma((2, n)),
            dma((2, n)),
            dma,
            dma,
            dma((7,)),
        ],
        compiler_params=pltpu.CompilerParams(
            collective_id=0, has_side_effects=True, vmem_limit_bytes=56 * 1024 * 1024
        ),
    )(plan, step_sizes, trajectory[0], modulation.transpose(0, 2, 1, 3), q_gain, k_gain, tile_mask.transpose(1, 2, 0), jnp.asarray(cosine), jnp.asarray(sine))
    result = pl.pallas_call(
        widen,
        out_shape=jax.ShapeDtypeStruct((B, LOC, D), F32),
        in_specs=[pl.BlockSpec(memory_space=pl.ANY)],
        out_specs=pl.BlockSpec(memory_space=pl.ANY),
        scratch_shapes=[pltpu.VMEM((B, LOC, D), BF16), pltpu.VMEM((B, LOC, D), F32), dma((B,)), dma((B,))],
        compiler_params=pltpu.CompilerParams(vmem_limit_bytes=56 * 1024 * 1024),
    )(blocks)
    return result[None]


def solution(mesh):
    placed = (P("tm", None, "seq", None), P("tm"), P("tm"), P(), P(), P(), P())
    return jax.shard_map(
        body, mesh=mesh, in_specs=placed, out_specs=P("tm", None, "seq", None), check_vma=False
    )
```
